512 devices in a mesh: tile: 64 (over z, x), member: 8 (over y, core).
Axes of the slice: x: 4, y: 4, z: 16, core: 2. Of those that a mesh axis runs over, the one named last changes fastest.
Arguments:
- cells: bfloat16 [8, 256, 4, 16, 256], P('member', 'tile'), may hold values from -6 to 6
- cotangent: bfloat16 [8, 256, 4, 16, 256], P('member', 'tile'), may hold values from -6 to 6
- slot_lats: int32 [64, 4], P('tile'), may hold values from 0 to 7, as said below
- slot_count: int32 [64], P('tile'), may hold values from 1 to 4, as said below
- kernel: float32 [7, 7, 256], replicated, may hold values from -0.875 to 0.875
- ln_gain: float32 [256], replicated, may hold values from 0.5 to 1.5
- w_in: bfloat16 [256, 1024], P(None, 'member'), may hold values from -0.375 to 0.375
- b_in: bfloat16 [1024], P('member'), may hold values from -4 to 4
- w_out: bfloat16 [1024, 256], P('member'), may hold values from -0.1875 to 0.1875
- layer_scale: float32 [256], replicated, may hold values from 0.5 to 1.5
Outputs:
- blocked: bfloat16 [8, 256, 4, 16, 256], P('member', 'tile')
- cell_grad: bfloat16 [8, 256, 4, 16, 256], P('member', 'tile')
- grad_in: float32 [256, 1024], P(None, 'member')
- grad_out: float32 [1024, 256], P('member')
- kernel_grad: float32 [7, 7, 256], replicated
The draws below stay inside these ranges and needn't reach their ends.
Inputs may be any that keep to these rules, and one draw needn't show every extreme that they name: `slot_lats`: row t lists 4 different tile rows of the grid; its first slot_count[t] entries are the wet tiles of tile column t. `slot_count`: some tile column has 4 wet tiles.
All inputs are finite; a program needn't handle non-finite values.
Results may differ from the reference program's by a relative error of at most 0.01.
Values may be sent and summed in bfloat16 or wider, within the bound.
A program may use at most 64 MiB of HBM per device.

```python
import math
import jax
import jax.numpy as jnp
from jax import lax

C = 256
FF = 1024
KS = 7
TH = 4
TW = 16
CAP = 4
GY = 8
NCOL = 64
SLOTS = 256
MEMBERS = 8


def column_table(key):
    base = jax.random.fold_in(key, 11)
    perm_key, count_key, pick_key = jax.random.split(base, 3)
    keys_all = jax.random.split(perm_key, NCOL)
    lats_all = jax.vmap(lambda column_key: jax.random.permutation(column_key, GY)[:CAP])(keys_all)
    counts = jax.random.randint(count_key, (NCOL,), 1, CAP + 1)
    chosen = jax.random.randint(pick_key, (), 0, NCOL)
    counts = jnp.where(jnp.arange(NCOL) == chosen, CAP, counts)
    return (lats_all.astype(jnp.int32), counts.astype(jnp.int32))


def draw_slot_lats(key, part):
    return column_table(key)[0]


def draw_slot_count(key, part):
    return column_table(key)[1]


def level_of(stream_key, shape, shards, smallest, top_value):
    level, own = 1.0, jax.random.fold_in(stream_key, 6)
    for axis_at, shards_of in shards:
        steps = jnp.exp(jax.random.uniform(jax.random.fold_in(own, axis_at), (shards_of,), jnp.float32, smallest / len(shards), top_value / len(shards)))
        level = level * jnp.repeat(steps, shape[axis_at] // shards_of).reshape([-1 if axis == axis_at else 1 for axis in range(len(shape))])
    return level


def bell_draw(rng, extent, scale, most, cuts=(), kind=jnp.bfloat16):
    drawn = scale * jax.random.normal(rng, extent, jnp.float32)
    if cuts:
        drawn = drawn * level_of(rng, extent, cuts, -0.22, 0.18)
    return jnp.clip(drawn, -most, most).astype(kind)


def setup_inputs(seed: int = 0) -> dict:
    key_list = jax.random.split(jax.random.key(seed), 11)
    cells = bell_draw(key_list[0], (MEMBERS, SLOTS, TH, TW, C), 1.0, 6.0, ((0, 8), (1, 64)))
    cotangent = bell_draw(key_list[1], (MEMBERS, SLOTS, TH, TW, C), 1.0, 6.0, ((0, 8), (1, 64)))
    slot_lats = draw_slot_lats(jax.random.fold_in(key_list[10], 71), 0)
    slot_count = draw_slot_count(jax.random.fold_in(key_list[10], 71), 0)
    kernel = bell_draw(key_list[4], (KS, KS, C), (KS * KS) ** -0.5, 0.875, (), jnp.float32)
    ln_gain = jnp.clip(jax.random.uniform(key_list[5], (C,), jnp.float32, 0.5, 1.5), 0.5, 1.5)
    w_in = bell_draw(key_list[6], (C, FF), C ** -0.5, 0.375, ((1, 8),))
    b_in = bell_draw(key_list[7], (FF,), 0.7, 4.0, ((0, 8),))
    w_out = bell_draw(key_list[8], (FF, C), FF ** -0.5, 0.1875, ((0, 8),))
    layer_scale = jnp.clip(jax.random.uniform(key_list[9], (C,), jnp.float32, 0.5, 1.5), 0.5, 1.5)
    return dict(cells=cells, cotangent=cotangent, slot_lats=slot_lats, slot_count=slot_count, kernel=kernel, ln_gain=ln_gain, w_in=w_in, b_in=b_in, w_out=w_out, layer_scale=layer_scale)


epsilon = 1e-06

def gelu_parts(hidden):
    cumulative = 0.5 * (1.0 + lax.erf(hidden * 0.7071067811865476))
    density = jnp.exp(-0.5 * hidden * hidden) * 0.3989422804014327
    return (hidden * cumulative, cumulative + hidden * density)

def depthwise(padded, kernel, height, breadth, flipped):
    span = kernel.shape[0]
    axis_row = padded.ndim - 3
    total = jnp.zeros(padded.shape[:-3] + (height, breadth, padded.shape[-1]), jnp.float32)
    for row_tap in range(span):
        rows_cut = lax.slice_in_dim(padded, row_tap, row_tap + height, axis=axis_row)
        for col_tap in range(span):
            window = lax.slice_in_dim(rows_cut, col_tap, col_tap + breadth, axis=axis_row + 1)
            if flipped:
                weight = kernel[span - 1 - row_tap, span - 1 - col_tap]
            else:
                weight = kernel[row_tap, col_tap]
            total = total + window.astype(jnp.float32) * weight
    return total

def kernel_taps(padded, gradient, height, breadth, span, axes_sum):
    axis_row = padded.ndim - 3
    rows_list = []
    for row_tap in range(span):
        rows_cut = lax.slice_in_dim(padded, row_tap, row_tap + height, axis=axis_row)
        cols_list = []
        for col_tap in range(span):
            window = lax.slice_in_dim(rows_cut, col_tap, col_tap + breadth, axis=axis_row + 1)
            cols_list.append(lax.optimization_barrier(jnp.sum(window.astype(jnp.float32) * gradient, axis=axes_sum)))
        rows_list.append(jnp.stack(cols_list))
    return jnp.stack(rows_list)

def mixing(conv_out, cells, cotangent, live_rows, ln_gain, w_in, b_in, w_out, layer_scale):
    channels = conv_out.shape[-1]
    layout = conv_out.shape
    flattened = conv_out.reshape(-1, channels)
    center = flattened - lax.optimization_barrier(jnp.mean(flattened, axis=-1, keepdims=True))
    inverse = lax.rsqrt(lax.optimization_barrier(jnp.mean(center * center, axis=-1, keepdims=True)) + epsilon)
    normed = center * inverse
    scaled = (normed * ln_gain).astype(jnp.bfloat16)
    hidden = jnp.dot(scaled, w_in, preferred_element_type=jnp.float32) + b_in.astype(jnp.float32)
    active, derivative = gelu_parts(hidden)
    active = active.astype(jnp.bfloat16)
    branch = jnp.dot(active, w_out, preferred_element_type=jnp.float32)
    blocked = (cells.reshape(-1, channels).astype(jnp.float32) + layer_scale * branch) * live_rows
    d_branch = (cotangent.reshape(-1, channels).astype(jnp.float32) * layer_scale * live_rows).astype(jnp.bfloat16)
    d_active = jnp.dot(d_branch, w_out.T, preferred_element_type=jnp.float32)
    grad_out = jnp.dot(active.T, d_branch, preferred_element_type=jnp.float32)
    d_hidden = (d_active * derivative).astype(jnp.bfloat16)
    grad_in = jnp.dot(scaled.T, d_hidden, preferred_element_type=jnp.float32)
    d_normed = jnp.dot(d_hidden, w_in.T, preferred_element_type=jnp.float32) * ln_gain
    d_conv = inverse * (d_normed - lax.optimization_barrier(jnp.mean(d_normed, axis=-1, keepdims=True)) - normed * lax.optimization_barrier(jnp.mean(d_normed * normed, axis=-1, keepdims=True)))
    return (blocked.astype(jnp.bfloat16).reshape(layout), d_conv.astype(jnp.bfloat16).reshape(layout), grad_in, grad_out)

def reference(cells, cotangent, slot_lats, slot_count, kernel, ln_gain, w_in, b_in, w_out, layer_scale):
    reach = KS // 2
    slot_ids = jnp.arange(CAP, dtype=jnp.int32)
    live = slot_ids[None, :] < slot_count[:, None]
    grid_rows = jnp.arange(GY, dtype=jnp.int32)
    onehot = ((grid_rows[None, :, None] == slot_lats[:, None, :]) & live[:, None, :]).astype(jnp.float32)
    live_mask = live.reshape(SLOTS)[:, None, None, None]
    live_rows = jnp.broadcast_to(live_mask, (SLOTS, TH, TW, 1)).astype(jnp.float32).reshape(-1, 1)
    total_rows = GY * TH
    total_cols = NCOL * TW

    def to_grid(values):
        pieces = values.astype(jnp.float32).reshape(NCOL, CAP, TH, TW, C)
        grid = jnp.einsum('dgs,dshwc->ghdwc', onehot, pieces)
        return grid.reshape(total_rows, total_cols, C)

    def from_grid(grid):
        pieces = grid.reshape(GY, TH, NCOL, TW, C)
        return jnp.einsum('dgs,ghdwc->dshwc', onehot, pieces).reshape(SLOTS, TH, TW, C)

    def pad_grid(grid):
        wrapped = jnp.concatenate([grid[:, total_cols - reach:], grid, grid[:, :reach]], axis=1)
        return jnp.pad(wrapped, ((reach, reach), (0, 0), (0, 0)))

    def member_step(totals, inputs):
        member_cells, member_cot = inputs
        grid_x = pad_grid(to_grid(member_cells))
        conv_out = from_grid(depthwise(grid_x, kernel, total_rows, total_cols, False))
        blocked, d_conv, grad_in, grad_out = mixing(conv_out, member_cells, member_cot, live_rows, ln_gain, w_in, b_in, w_out, layer_scale)
        grid_dy = to_grid(d_conv)
        back = from_grid(depthwise(pad_grid(grid_dy), kernel, total_rows, total_cols, True))
        cell_grad = jnp.where(live_mask, member_cot.astype(jnp.float32) + back, 0.0).astype(jnp.bfloat16)
        taps = kernel_taps(grid_x, grid_dy, total_rows, total_cols, KS, (0, 1))
        return ((totals[0] + grad_in, totals[1] + grad_out, totals[2] + taps), (blocked, cell_grad))
    start = (jnp.zeros((C, FF), jnp.float32), jnp.zeros((FF, C), jnp.float32), jnp.zeros((KS, KS, C), jnp.float32))
    totals, outputs = lax.scan(member_step, start, (cells, cotangent))
    factor = 1.0 / math.sqrt(MEMBERS * SLOTS * TH * TW)
    return (outputs[0], outputs[1], totals[0] * factor, totals[1] * factor, totals[2] * factor)
```

```python
import functools
import math

import jax
import jax.numpy as jnp
from jax import lax
from jax.experimental import pallas as pl
from jax.experimental.pallas import tpu as pltpu
from jax.sharding import PartitionSpec as P

NZ, NX, NY, NC = 16, 4, 4, 2
NL, NH = 4, 4
SLOTS, GY, TH, TW, KS = 4, 8, 4, 16, 7
REACH = KS // 2
LEFT = 8
ROWS = GY * TH
EPSILON = 1e-06
MESH = pl.DeviceIdType.MESH
F32, BF16 = jnp.float32, jnp.bfloat16
ORDER = (0, 1, 3, 2)
PEERS = 1 + 15 + 3 + 3 + 3 + 9 + 2

VMEM_SCRATCH = dict(
    grid_x=((ROWS + 2 * REACH, 32, 256), F32),
    grid_d=((ROWS + 2 * REACH, 32, 256), F32),
    edge=((2, 96, 256), F32),
    edge_x_out=((2, 96, 256), BF16),
    edge_x_in=((2, 96, 256), BF16),
    edge_d_out=((2, 96, 256), BF16),
    edge_d_in=((2, 96, 256), BF16),
    wi=((NY, 256, 256), BF16),
    wo=((NY, 256, 256), BF16),
    bias_own=((8, 128), F32),
    bias=((NY, 8, 256), F32),
    normed=((SLOTS, TH, TW, 256), F32),
    inverse=((SLOTS, TH, TW, 128), F32),
    scaled=((SLOTS, TH, TW, 256), BF16),
    d_branch=((SLOTS, TH, TW, 256), BF16),
    branch=((256, 256), F32),
    d_normed=((256, 256), F32),
    d_conv=((SLOTS, TH, TW, 256), F32),
    g_in=((NY, 256, 256), BF16),
    g_out=((NY, 256, 256), BF16),
    core_in=((NY, 256, 128), BF16),
    core_out=((NY, 128, 256), BF16),
    piece=((NY, NX, 128, 128), BF16),
    piece_in=((NY * NX, 128, 128), BF16),
    low_out=((NL, 32, 128), BF16),
    low_in=((NL, 32, 128), BF16),
    high=((NH, 32, 128), BF16),
    full=((NX, NL, 32, 128), BF16),
    taps=((NC, NY, 16, 128), F32),
    taps_core=((NY, 16, 128), F32),
    taps_sum=((NY, 16, 128), F32),
    taps_plane=((NY * NX, 16, 128), F32),
    taps_low=((NL, 16, 128), F32),
    taps_high=((NH, 16, 128), F32),
    taps_full=((NY * NC, 16, 128), F32),
)
DMA_COUNTS = dict(
    ex=2, ed=2, wy=9, wc=12, gc=8, gp=16, gl=4, gh=4, gg=16, kc=1, kp=16, kl=4, kh=4, km=8
)
INPUTS = (
    "cells", "cot", "lats", "count", "kernel", "gain", "w_in", "b_in", "w_out", "scale"
)
OUTPUTS = ("blocked", "cell_grad", "grad_in", "grad_out", "kernel_grad")


class Refs:
    pass


def gelu_parts(hidden):
    cumulative = 0.5 * (1.0 + lax.erf(hidden * 0.7071067811865476))
    density = jnp.exp(-0.5 * hidden * hidden) * 0.3989422804014327
    return (hidden * cumulative, cumulative + hidden * density)


def dot(a, b, contract):
    return lax.dot_general(a, b, ((contract[0:1], contract[1:2]), ((), ())), preferred_element_type=F32)


def block_kernel(factor, *refs):
    r = Refs()
    names = INPUTS + OUTPUTS + tuple(VMEM_SCRATCH)
    for name, ref in zip(names, refs):
        setattr(r, name, ref)
    sems = {}
    rest = refs[len(names):]
    for index, name in enumerate(DMA_COUNTS):
        sems[name] = (rest[2 * index], rest[2 * index + 1])

    t, m = lax.axis_index("tile"), lax.axis_index("member")
    z, x, y, c = t // NX, t % NX, m // NC, m % NC
    zh, zl = z // NL, z % NL
    sends = []

    def at(zz, xx, yy, cc):
        return {"tile": zz * NX + xx, "member": yy * NC + cc}

    def plane(dy, dx):
        return at(z, (x + dx) % NX, (y + dy) % NY, c)

    def low(dl, dx=0):
        return at(zh * NL + (zl + dl) % NL, (x + dx) % NX, y, c)

    def high(dh):
        return at((zh + dh) % NH * NL + zl, x, y, c)

    def member(index):
        return at(z, x, (y + index // NC) % NY, (c + index) % NC)

    def remote(src, dst, name, index, target):
        return pltpu.make_async_remote_copy(
            src_ref=src,
            dst_ref=dst,
            send_sem=sems[name][0].at[index],
            recv_sem=sems[name][1].at[index],
            device_id=target,
            device_id_type=MESH,
        )

    def send(*copy):
        made = remote(*copy)
        made.start()
        sends.append(made)
        return made

    left = {"tile": (t + NZ * NX - 1) % (NZ * NX), "member": m}
    right = {"tile": (t + 1) % (NZ * NX), "member": m}
    sibling = at(z, x, y, 1 - c)

    barrier = pltpu.get_barrier_semaphore()

    def greet(target):
        pl.semaphore_signal(barrier, inc=1, device_id=target, device_id_type=MESH)

    for dh in range(1, NH):
        greet(high(dh))
    greet(left)
    greet(right)
    greet(sibling)
    for step in range(1, 16):
        greet(plane(step // 4, step % 4))
    for dy in range(1, NY):
        greet(at(z, x, (y + dy) % NY, 1 - c))
    for dl in range(1, NL):
        for dx in range(NX):
            greet(low(dl, dx))

    def live(s):
        return jnp.where(s < r.count[0], 1.0, 0.0).astype(F32)

    def place(grid, values):
        grid[...] = jnp.zeros_like(grid)

        @pl.loop(0, GY)
        def _(g):
            found, weight = jnp.int32(0), jnp.float32(0.0)
            for s in range(SLOTS):
                hit = jnp.where(r.lats[0, s] == g, 1, 0)
                found += hit * s
                weight += hit.astype(F32) * live(s)
            tile = values[jnp.minimum(found, SLOTS - 1)].astype(F32) * weight
            grid[pl.ds(REACH + g * TH, TH), LEFT:LEFT + TW, :] = tile

    def send_edges(grid, out, landing, name):
        for row in range(ROWS):
            spot = slice(3 * row, 3 * row + 3)
            r.edge[0, spot, :] = grid[REACH + row, LEFT:LEFT + 3, :]
            r.edge[1, spot, :] = grid[REACH + row, LEFT + TW - 3:LEFT + TW, :]
        out[...] = r.edge[...].astype(BF16)

    def edge_copies(out, landing, name):
        return (
            (out.at[0], landing.at[1], name, 0, left),
            (out.at[1], landing.at[0], name, 1, right),
        )

    def take_edges(grid, landing):
        r.edge[...] = landing[...].astype(F32)
        for row in range(ROWS):
            spot = slice(3 * row, 3 * row + 3)
            grid[REACH + row, LEFT - 3:LEFT, :] = r.edge[0, spot, :]
            grid[REACH + row, LEFT + TW:LEFT + TW + 3, :] = r.edge[1, spot, :]

    def depthwise(grid, s, flipped):
        base = r.lats[0, s] * TH
        total = [jnp.zeros((TW, 256), F32) for _ in range(TH)]
        for b in range(KS):
            for i in range(TH + 2 * REACH):
                window = grid[base + i, LEFT - REACH + b:LEFT - REACH + b + TW, :]
                for a in range(KS):
                    if 0 <= i - a < TH:
                        ka, kb = (KS - 1 - a, KS - 1 - b) if flipped else (a, b)
                        total[i - a] += window * r.kernel[ka, kb:kb + 1, :]
        return total

    r.bias_own[...] = jnp.broadcast_to(r.b_in[...].astype(F32), (8, 128))
    lanes = pl.ds(pl.multiple_of(c * 128, 128), 128)
    other_lanes = pl.ds(pl.multiple_of((1 - c) * 128, 128), 128)
    r.wi[y, :, lanes] = r.w_in[...]
    r.wo[y, lanes, :] = r.w_out[...]
    r.bias[y, :, lanes] = r.bias_own[...]
    place(r.grid_x, r.cells)
    send_edges(r.grid_x, r.edge_x_out, r.edge_x_in, "ex")

    pl.semaphore_wait(barrier, PEERS)

    edges = [send(*copy) for copy in edge_copies(r.edge_x_out, r.edge_x_in, "ex")]

    def weights(yy):
        return (
            r.wi.at[yy, :, lanes],
            r.wo.at[yy, lanes, :],
            r.bias.at[yy, :, lanes],
        )

    def weights_other(yy):
        return (
            r.wi.at[yy, :, other_lanes],
            r.wo.at[yy, other_lanes, :],
            r.bias.at[yy, :, other_lanes],
        )

    for dy in (2, 1, 3):
        for kind, part in enumerate(weights(y)):
            send(part, part, "wy", (dy - 1) * 3 + kind, plane(dy, 0))
    for kind, part in enumerate(weights(y)):
        send(part, part, "wc", kind, sibling)

    def forward_weights(dy):
        yy = (y + NY - dy) % NY
        for kind, part in enumerate(weights(yy)):
            remote(part, part, "wy", (dy - 1) * 3 + kind, plane(dy, 0)).wait_recv()
            send(part, part, "wc", dy * 3 + kind, sibling)

    for s in range(SLOTS):
        r.d_branch[s] = (
            r.cot[s].astype(F32) * (r.scale[...] * live(s))
        ).astype(BF16)
    r.branch[...] = jnp.zeros_like(r.branch)
    r.d_normed[...] = jnp.zeros_like(r.d_normed)

    for copy in edges:
        copy.wait_recv()
    take_edges(r.grid_x, r.edge_x_in)
    forward_weights(1)
    forward_weights(3)

    @pl.loop(0, SLOTS)
    def _(s):
        total = depthwise(r.grid_x, s, False)
        for row in range(TH):
            center = total[row] - jnp.mean(total[row], axis=-1, keepdims=True)
            inverse = lax.rsqrt(jnp.mean(center * center, axis=-1, keepdims=True) + EPSILON)
            normed = center * inverse
            r.normed[s, row] = normed
            r.inverse[s, row] = jnp.broadcast_to(inverse, (TW, 128))
            r.scaled[s, row] = (normed * r.gain[...]).astype(BF16)

    forward_weights(2)

    def pair(dy):
        yy = (y + NY - dy) % NY
        for kind, part in enumerate(weights_other(yy)):
            remote(part, part, "wc", dy * 3 + kind, sibling).wait_recv()
        scaled = r.scaled[...].reshape(256, 256)
        d_branch = r.d_branch[...].reshape(256, 256)
        hidden = dot(scaled, r.wi[yy], (1, 0)) + r.bias[yy, 0:1, :]
        active, derivative = gelu_parts(hidden)
        active = active.astype(BF16)
        r.branch[...] += dot(active, r.wo[yy], (1, 0))
        r.g_out[dy] = dot(active, d_branch, (0, 0)).astype(BF16)
        d_active = dot(d_branch, r.wo[yy], (1, 1))
        d_hidden = (d_active * derivative).astype(BF16)
        r.g_in[dy] = dot(scaled, d_hidden, (0, 0)).astype(BF16)
        to_core = [
            send(r.g_in.at[dy, :, other_lanes], r.core_in.at[dy], "gc", dy * 2, sibling),
            send(r.g_out.at[dy, other_lanes, :], r.core_out.at[dy], "gc", dy * 2 + 1, sibling),
        ]
        r.d_normed[...] += dot(d_hidden, r.wi[yy], (1, 1))
        return to_core

    def spread(dy, to_core):
        back = (NY - dy) % NY
        to_core[0].wait_recv()
        g_in = r.g_in[dy, :, lanes].astype(F32) + r.core_in[dy].astype(F32)
        r.piece[dy, 0] = g_in[:128].astype(BF16)
        r.piece[dy, 1] = g_in[128:].astype(BF16)
        to_core[1].wait_recv()
        g_out = r.g_out[dy, lanes, :].astype(F32) + r.core_out[dy].astype(F32)
        r.piece[dy, 2] = g_out[:, :128].astype(BF16)
        r.piece[dy, 3] = g_out[:, 128:].astype(BF16)
        for dx in (2, 1, 3, 0):
            if dy or dx:
                index = back * 4 + dx
                send(r.piece.at[dy, (x + dx) % NX], r.piece_in.at[index], "gp", index, plane(back, dx))

    held = None
    for dy in ORDER:
        now = (dy, pair(dy))
        if held is not None:
            spread(*held)
        held = now

    for s in range(SLOTS):
        d_normed = r.d_normed[s * 64:(s + 1) * 64, :] * r.gain[...]
        normed = r.normed[s].reshape(64, 256)
        mean = jnp.mean(d_normed, axis=-1, keepdims=True)
        along = jnp.mean(d_normed * normed, axis=-1, keepdims=True)
        inverse = r.inverse[s].reshape(64, 128)[:, 0:1]
        d_conv = inverse * (d_normed - mean - normed * along)
        r.d_conv[s] = d_conv.astype(BF16).astype(F32).reshape(TH, TW, 256)
    place(r.grid_d, r.d_conv)
    send_edges(r.grid_d, r.edge_d_out, r.edge_d_in, "ed")
    edges = [send(*copy) for copy in edge_copies(r.edge_d_out, r.edge_d_in, "ed")]
    spread(*held)

    for b in range(KS):
        def slot_taps(s, sums):
            sums = list(sums)
            base = r.lats[0, s] * TH
            for i in range(TH + 2 * REACH):
                window = r.grid_x[base + i, LEFT - REACH + b:LEFT - REACH + b + TW, :]
                for a in range(KS):
                    if 0 <= i - a < TH:
                        product = window * r.d_conv[s, i - a]
                        sums[a] += product[:8] + product[8:]
            return tuple(sums)

        sums = lax.fori_loop(
            0, SLOTS, slot_taps, tuple(jnp.zeros((8, 256), F32) for _ in range(KS))
        )
        for a in range(KS):
            line = jnp.sum(sums[a], axis=0, keepdims=True)
            for half in range(2):
                at_row = 2 * (a * KS + b) + half
                owner = at_row // 16
                r.taps[owner % NC, owner // NC, at_row % 16:at_row % 16 + 1, :] = (
                    line[:, half * 128:(half + 1) * 128]
                )
    for at_row in range(2 * KS * KS, 128):
        owner = at_row // 16
        r.taps[owner % NC, owner // NC, at_row % 16:at_row % 16 + 1, :] = jnp.zeros((1, 128), F32)
    k_core = send(r.taps.at[1 - c], r.taps_core, "kc", 0, sibling)
    for s in range(SLOTS):
        r.blocked[s] = (
            (r.cells[s].astype(F32) + r.scale[...] * r.branch[s * 64:(s + 1) * 64, :].reshape(TH, TW, 256))
            * live(s)
        ).astype(BF16)
    k_core.wait_recv()
    r.taps_sum[...] = r.taps[c] + r.taps_core[...]
    spot = y * NX + x
    r.taps_plane[spot] = r.taps_sum[y]
    for step in range(1, 16):
        dy, dx = step // 4, step % 4
        send(r.taps_sum.at[(y + dy) % NY], r.taps_plane.at[spot], "kp", step, plane(dy, dx))

    own = r.piece[0, x].astype(F32)
    for step in range(1, 16):
        remote(
            r.piece.at[0, 0], r.piece_in.at[step], "gp", step, plane(step // 4, step % 4)
        ).wait_recv()
        own += r.piece_in[step].astype(F32)
    r.low_out[...] = own.astype(BF16).reshape(NL, 32, 128)
    for dl in (2, 1, 3):
        send(r.low_out.at[(zl + dl) % NL], r.low_in.at[dl], "gl", dl, low(dl))

    for copy in edges:
        copy.wait_recv()
    take_edges(r.grid_d, r.edge_d_in)

    for step in range(1, 16):
        dy, dx = step // 4, step % 4
        origin = (y + NY - dy) % NY * NX + (x + NX - dx) % NX
        remote(r.taps_sum.at[0], r.taps_plane.at[origin], "kp", step, plane(dy, dx)).wait_recv()
    r.taps_low[zl] = jnp.sum(r.taps_plane[...], axis=0)
    for dl in (2, 1, 3):
        send(r.taps_low.at[zl], r.taps_low.at[zl], "kl", dl, low(dl))

    own = r.low_out[zl].astype(F32)
    for dl in range(1, NL):
        remote(r.low_out.at[0], r.low_in.at[dl], "gl", dl, low(dl)).wait_recv()
        own += r.low_in[dl].astype(F32)
    r.high[zh] = own.astype(BF16)
    for dh in (2, 1, 3):
        send(r.high.at[zh], r.high.at[zh], "gh", dh, high(dh))

    @pl.loop(0, SLOTS)
    def _(s):
        total = depthwise(r.grid_d, s, True)
        for row in range(TH):
            r.cell_grad[s, row] = (
                (r.cot[s, row].astype(F32) + total[row]) * live(s)
            ).astype(BF16)

    for dl in range(1, NL):
        origin = (zl + NL - dl) % NL
        remote(r.taps_low.at[0], r.taps_low.at[origin], "kl", dl, low(dl)).wait_recv()
    r.taps_high[zh] = jnp.sum(r.taps_low[...], axis=0)
    for dh in (2, 1, 3):
        send(r.taps_high.at[zh], r.taps_high.at[zh], "kh", dh, high(dh))

    for dh in range(1, NH):
        origin = (zh + NH - dh) % NH
        remote(r.high.at[0], r.high.at[origin], "gh", dh, high(dh)).wait_recv()
    r.full[x, zl] = (jnp.sum(r.high[...].astype(F32), axis=0) * factor).astype(BF16)
    for step in range(1, 16):
        dl, dx = step // 4, step % 4
        send(r.full.at[x, zl], r.full.at[x, zl], "gg", step, low(dl, dx))

    for dh in range(1, NH):
        origin = (zh + NH - dh) % NH
        remote(r.taps_high.at[0], r.taps_high.at[origin], "kh", dh, high(dh)).wait_recv()
    r.taps_full[m] = jnp.sum(r.taps_high[...], axis=0) * factor
    for index in range(1, 8):
        send(r.taps_full.at[m], r.taps_full.at[m], "km", index, member(index))

    for step in range(1, 16):
        dl, dx = step // 4, step % 4
        remote(
            r.full.at[0, 0],
            r.full.at[(x + NX - dx) % NX, (zl + NL - dl) % NL],
            "gg",
            step,
            low(dl, dx),
        ).wait_recv()
    for half in range(2):
        r.grad_in[half * 128:(half + 1) * 128, :] = r.full[half].reshape(128, 128).astype(F32)
        r.grad_out[:, half * 128:(half + 1) * 128] = (
            r.full[2 + half].reshape(128, 128).astype(F32)
        )
    for index in range(1, 8):
        origin = (y + NY - index // NC) % NY * NC + (c + index) % NC
        remote(r.taps_full.at[0], r.taps_full.at[origin], "km", index, member(index)).wait_recv()
    for a in range(KS):
        for b in range(KS):
            for half in range(2):
                at_row = 2 * (a * KS + b) + half
                r.kernel_grad[a, b:b + 1, half * 128:(half + 1) * 128] = (
                    r.taps_full[at_row // 16, at_row % 16:at_row % 16 + 1, :]
                )
    for copy in sends:
        copy.wait_send()


def on_device(
    cells, cotangent, slot_lats, slot_count, kernel, ln_gain, w_in, b_in, w_out, layer_scale
):
    cell_count = 8 * 256 * TH * TW
    factor = 1.0 / math.sqrt(cell_count)
    vmem = pl.BlockSpec(memory_space=pltpu.VMEM)
    smem = pl.BlockSpec(memory_space=pltpu.SMEM)
    tiles = jax.ShapeDtypeStruct((SLOTS, TH, TW, 256), BF16)
    blocked, cell_grad, grad_in, grad_out, kernel_grad = pl.pallas_call(
        functools.partial(block_kernel, factor),
        out_shape=(
            tiles,
            tiles,
            jax.ShapeDtypeStruct((256, 128), F32),
            jax.ShapeDtypeStruct((128, 256), F32),
            jax.ShapeDtypeStruct((KS, KS, 256), F32),
        ),
        in_specs=[vmem, vmem, smem, smem] + [vmem] * 6,
        out_specs=[vmem] * 5,
        scratch_shapes=[pltpu.VMEM(*spec) for spec in VMEM_SCRATCH.values()]
        + [pltpu.SemaphoreType.DMA((n,)) for n in DMA_COUNTS.values() for _ in range(2)],
        compiler_params=pltpu.CompilerParams(
            collective_id=0, has_side_effects=True, vmem_limit_bytes=40 * 1024 * 1024
        ),
        name="block",
    )(
        cells[0],
        cotangent[0],
        slot_lats,
        slot_count,
        kernel,
        ln_gain.reshape(1, 256),
        w_in,
        b_in.reshape(1, 128),
        w_out,
        layer_scale.reshape(1, 256),
    )
    return blocked[None], cell_grad[None], grad_in, grad_out, kernel_grad


def solution(mesh):
    placed = (
        P("member", "tile", None, None, None),
        P("member", "tile", None, None, None),
        P("tile", None),
        P("tile"),
        P(),
        P(),
        P(None, "member"),
        P("member"),
        P("member", None),
        P(),
    )
    return jax.shard_map(
        on_device,
        mesh=mesh,
        in_specs=placed,
        out_specs=(
            P("member", "tile", None, None, None),
            P("member", "tile", None, None, None),
            P(None, "member"),
            P("member", None),
            P(),
        ),
        check_vma=False,
    )
```

```python
import functools
import math

import jax
import jax.numpy as jnp
from jax import lax
from jax.experimental import pallas as pl
from jax.experimental.pallas import tpu as pltpu
from jax.sharding import PartitionSpec as P

NZ, NX, NY, NC = 16, 4, 4, 2
NL, NH = 4, 4
SLOTS, GY, TH, TW, KS = 4, 8, 4, 16, 7
REACH = KS // 2
LEFT = 8
ROWS = GY * TH
EPSILON = 1e-06
MESH = pl.DeviceIdType.MESH
F32, BF16 = jnp.float32, jnp.bfloat16
ORDER = (1, 3, 2, 0)
PEERS = 6 + 2 + 6 + 3 + 1

VMEM_SCRATCH = dict(
    cells=((SLOTS, TH, TW, 256), BF16),
    cot=((SLOTS, TH, TW, 256), BF16),
    kernel=((KS, KS, 256), F32),
    w_in=((256, 128), BF16),
    w_out=((128, 256), BF16),
    blocked=((SLOTS, TH, TW, 256), BF16),
    cell_grad=((SLOTS, TH, TW, 256), BF16),
    grad_in=((256, 128), F32),
    grad_out=((128, 256), F32),
    kernel_grad=((KS, KS, 256), F32),
    strip=((ROWS + 2 * REACH, 16, 256), F32),
    pair_taps=((KS, REACH, 8, 256), F32),
    conv=((SLOTS, TH, TW, 256), F32),
    grid_x=((ROWS + 2 * REACH, 32, 256), F32),
    grid_d=((ROWS + 2 * REACH, 32, 256), F32),
    edge=((2, 96, 256), F32),
    edge_x_out=((2, 96, 256), BF16),
    edge_x_in=((2, 96, 256), BF16),
    edge_d_out=((2, 96, 256), BF16),
    edge_d_in=((2, 96, 256), BF16),
    wi=((NY, 256, 256), BF16),
    wo=((NY, 256, 256), BF16),
    bias_own=((8, 128), F32),
    bias=((NY, 8, 256), F32),
    normed=((SLOTS, TH, TW, 256), F32),
    inverse=((SLOTS, TH, TW, 128), F32),
    scaled=((SLOTS, TH, TW, 256), BF16),
    d_branch=((SLOTS, TH, TW, 256), BF16),
    branch=((256, 256), F32),
    d_normed=((256, 256), F32),
    d_conv=((SLOTS, TH, TW, 256), F32),
    g_in=((NY, 256, 256), BF16),
    g_out=((NY, 256, 256), BF16),
    core_in=((NY, 256, 128), BF16),
    core_out=((NY, 128, 256), BF16),
    piece=((NY, NX, 128, 128), BF16),
    piece_in=((NY * NX, 128, 128), BF16),
    low_out=((NL, 32, 128), BF16),
    low_in=((NL, 32, 128), BF16),
    high=((NH, 32, 128), BF16),
    full=((NX, NL, 32, 128), BF16),
    taps=((NC, NY, 16, 128), F32),
    taps_core=((NY, 16, 128), F32),
    taps_sum=((NY, 16, 128), F32),
    taps_plane=((NY * NX, 16, 128), F32),
    taps_low=((NL, 16, 128), F32),
    taps_high=((NH, 16, 128), F32),
    taps_full=((NY * NC, 16, 128), F32),
)
DMA_COUNTS = dict(
    ex=2, ed=2, wy=9, wc=12, gc=8, gp=16, gl=4, gh=4, gg=16, kc=1, kp=16, kl=4, kh=4, km=8
)
INPUTS = (
    "cells_far", "cot_far", "lats", "count", "kernel_far", "gain", "w_in_far", "b_in", "w_out_far", "scale"
)
LOCAL = ("cells", "w_in", "w_out", "kernel", "cot")
OUTPUTS = ("blocked", "cell_grad", "grad_in", "grad_out", "kernel_grad")
VMEM_BYTES = 62 * 1024 * 1024


class Refs:
    pass


def gelu_parts(hidden):
    cumulative = 0.5 * (1.0 + lax.erf(hidden * 0.7071067811865476))
    density = jnp.exp(-0.5 * hidden * hidden) * 0.3989422804014327
    return (hidden * cumulative, cumulative + hidden * density)


def dot(a, b, contract):
    return lax.dot_general(a, b, ((contract[0:1], contract[1:2]), ((), ())), preferred_element_type=F32)


def block_kernel(factor, *refs):
    r = Refs()
    names = INPUTS + tuple(name + "_far" for name in OUTPUTS) + tuple(VMEM_SCRATCH)
    for name, ref in zip(names, refs):
        setattr(r, name, ref)
    sems = {}
    rest = refs[len(names):]
    for index, name in enumerate(DMA_COUNTS):
        sems[name] = (rest[2 * index], rest[2 * index + 1])
    local_sems, result_sems, relay_1, relay_2 = rest[2 * len(DMA_COUNTS):]
    local = {}
    for index, name in enumerate(LOCAL):
        local[name] = pltpu.make_async_copy(
            getattr(r, name + "_far"), getattr(r, name), local_sems.at[index]
        )
        local[name].start()
    results = []

    def give(index):
        name = OUTPUTS[index]
        copy = pltpu.make_async_copy(
            getattr(r, name), getattr(r, name + "_far"), result_sems.at[index]
        )
        copy.start()
        results.append(copy)


    t, m = lax.axis_index("tile"), lax.axis_index("member")
    z, x, y, c = t // NX, t % NX, m // NC, m % NC
    zh, zl = z // NL, z % NL
    sends = []

    def at(zz, xx, yy, cc):
        return {"tile": zz * NX + xx, "member": yy * NC + cc}

    def plane(dy, dx):
        return at(z, (x + dx) % NX, (y + dy) % NY, c)

    def low(dl, dx=0):
        return at(zh * NL + (zl + dl) % NL, (x + dx) % NX, y, c)

    def high(dh):
        return at((zh + dh) % NH * NL + zl, x, y, c)

    def member(index):
        return at(z, x, (y + index // NC) % NY, (c + index) % NC)

    def remote(src, dst, name, index, target):
        return pltpu.make_async_remote_copy(
            src_ref=src,
            dst_ref=dst,
            send_sem=sems[name][0].at[index],
            recv_sem=sems[name][1].at[index],
            device_id=target,
            device_id_type=MESH,
        )

    def send(*copy):
        made = remote(*copy)
        made.start()
        sends.append(made)
        return made

    left = {"tile": (t + NZ * NX - 1) % (NZ * NX), "member": m}
    right = {"tile": (t + 1) % (NZ * NX), "member": m}
    sibling = at(z, x, y, 1 - c)

    barrier = pltpu.get_barrier_semaphore()

    def greet(target):
        pl.semaphore_signal(barrier, inc=1, device_id=target, device_id_type=MESH)

    def along(dz):
        return at((z + NZ + dz) % NZ, x, y, c)

    for dz in (3, -3, 2, -2, 1, -1):
        greet(along(dz))
    greet(left)
    greet(right)
    for dy in range(1, NY):
        greet(plane(dy, 0))
        greet(at(z, x, (y + dy) % NY, 1 - c))
    for dx in range(1, NX):
        greet(plane(0, dx))
    greet(sibling)

    def relay(semaphore, targets):
        for target in targets:
            pl.semaphore_signal(semaphore, inc=1, device_id=target, device_id_type=MESH)

    def live(s):
        return jnp.where(s < r.count[0], 1.0, 0.0).astype(F32)

    def place(grid, values):
        grid[...] = jnp.zeros_like(grid)

        @pl.loop(0, GY)
        def _(g):
            found, weight = jnp.int32(0), jnp.float32(0.0)
            for s in range(SLOTS):
                hit = jnp.where(r.lats[0, s] == g, 1, 0)
                found += hit * s
                weight += hit.astype(F32) * live(s)
            tile = values[jnp.minimum(found, SLOTS - 1)].astype(F32) * weight
            grid[pl.ds(REACH + g * TH, TH), LEFT:LEFT + TW, :] = tile

    def send_edges(grid, out, landing, name):
        for row in range(ROWS):
            spot = slice(3 * row, 3 * row + 3)
            r.edge[0, spot, :] = grid[REACH + row, LEFT:LEFT + 3, :]
            r.edge[1, spot, :] = grid[REACH + row, LEFT + TW - 3:LEFT + TW, :]
        out[...] = r.edge[...].astype(BF16)

    def edge_copies(out, landing, name):
        return (
            (out.at[0], landing.at[1], name, 0, left),
            (out.at[1], landing.at[0], name, 1, right),
        )

    def take_edges(grid, landing):
        r.edge[...] = landing[...].astype(F32)
        for row in range(ROWS):
            spot = slice(3 * row, 3 * row + 3)
            grid[REACH + row, LEFT - 3:LEFT, :] = r.edge[0, spot, :]
            grid[REACH + row, LEFT + TW:LEFT + TW + 3, :] = r.edge[1, spot, :]

    def depthwise(grid, s, flipped):
        base = r.lats[0, s] * TH
        total = [jnp.zeros((TW, 256), F32) for _ in range(TH)]
        for b in range(KS):
            for i in range(TH + 2 * REACH):
                window = grid[base + i, LEFT - REACH + b:LEFT - REACH + b + TW, :]
                for a in range(KS):
                    if 0 <= i - a < TH:
                        ka, kb = (KS - 1 - a, KS - 1 - b) if flipped else (a, b)
                        total[i - a] += window * r.kernel[ka, kb:kb + 1, :]
        return total

    r.bias_own[...] = jnp.broadcast_to(r.b_in[...].astype(F32), (8, 128))
    lanes = pl.ds(pl.multiple_of(c * 128, 128), 128)
    other_lanes = pl.ds(pl.multiple_of((1 - c) * 128, 128), 128)
    r.bias[y, :, lanes] = r.bias_own[...]
    local["cells"].wait()
    place(r.grid_x, r.cells)
    send_edges(r.grid_x, r.edge_x_out, r.edge_x_in, "ex")

    local["w_in"].wait()
    local["w_out"].wait()
    r.wi[y, :, lanes] = r.w_in[...]
    r.wo[y, lanes, :] = r.w_out[...]
    pl.semaphore_wait(barrier, PEERS)
    relay(
        relay_1,
        [plane(dy, 0) for dy in range(1, NY)]
        + [plane(0, dx) for dx in range(1, NX)]
        + [along(2), along(-2)],
    )

    edges = [send(*copy) for copy in edge_copies(r.edge_x_out, r.edge_x_in, "ex")]

    def weights(yy):
        return (
            r.wi.at[yy, :, lanes],
            r.wo.at[yy, lanes, :],
            r.bias.at[yy, :, lanes],
        )

    def weights_other(yy):
        return (
            r.wi.at[yy, :, other_lanes],
            r.wo.at[yy, other_lanes, :],
            r.bias.at[yy, :, other_lanes],
        )

    for dy in (1, 3, 2):
        for kind, part in enumerate(weights(y)):
            send(part, part, "wy", (dy - 1) * 3 + kind, plane(dy, 0))
    for kind, part in enumerate(weights(y)):
        send(part, part, "wc", kind, sibling)

    def forward_weights(dy):
        yy = (y + NY - dy) % NY
        for kind, part in enumerate(weights(yy)):
            remote(part, part, "wy", (dy - 1) * 3 + kind, plane(dy, 0)).wait_recv()
            send(part, part, "wc", dy * 3 + kind, sibling)

    local["kernel"].wait()
    low_half = lax.broadcasted_iota(jnp.int32, (8, 256), 0) < 4
    for a in range(KS):
        for b in range(REACH):
            r.pair_taps[a, b] = jnp.where(
                low_half, r.kernel[a, b:b + 1, :], r.kernel[a, b + 4:b + 5, :]
            )

    @pl.loop(0, SLOTS)
    def _(s):
        total = depthwise(r.grid_x, s, False)
        for row in range(TH):
            r.conv[s, row] = total[row]

    r.strip[...] = jnp.zeros_like(r.strip)
    local["cot"].wait()
    for s in range(SLOTS):
        r.d_branch[s] = (
            r.cot[s].astype(F32) * (r.scale[...] * live(s))
        ).astype(BF16)
    r.branch[...] = jnp.zeros_like(r.branch)
    r.d_normed[...] = jnp.zeros_like(r.d_normed)

    pl.semaphore_wait(relay_1, 8)
    relay(
        relay_2, [plane(0, dx) for dx in range(1, NX)] + [along(4), along(-4)]
    )
    for copy in edges:
        copy.wait_recv()
    r.edge[...] = r.edge_x_in[...].astype(F32)
    for row in range(ROWS):
        spot = slice(3 * row, 3 * row + 3)
        r.strip[REACH + row, 0:3, :] = r.edge[0, spot, :]
        r.strip[REACH + row, 7:10, :] = r.edge[1, spot, :]
    forward_weights(1)
    forward_weights(3)

    @pl.loop(0, SLOTS)
    def _(s):
        base = r.lats[0, s] * TH
        outer = [jnp.zeros((8, 256), F32) for _ in range(TH)]
        for b in range(REACH):
            for i in range(TH + 2 * REACH):
                window = r.strip[base + i, b:b + 8, :]
                for a in range(KS):
                    if 0 <= i - a < TH:
                        outer[i - a] += window * r.pair_taps[a, b]
        for row in range(TH):
            total = r.conv[s, row] + jnp.concatenate(
                [jnp.where(low_half, outer[row], 0.0), jnp.where(low_half, 0.0, outer[row])], axis=0
            )
            center = total - jnp.mean(total, axis=-1, keepdims=True)
            inverse = lax.rsqrt(jnp.mean(center * center, axis=-1, keepdims=True) + EPSILON)
            normed = center * inverse
            r.normed[s, row] = normed
            r.inverse[s, row] = jnp.broadcast_to(inverse, (TW, 128))
            r.scaled[s, row] = (normed * r.gain[...]).astype(BF16)

    def pair(dy):
        yy = (y + NY - dy) % NY
        for kind, part in enumerate(weights_other(yy)):
            remote(part, part, "wc", dy * 3 + kind, sibling).wait_recv()
        scaled = r.scaled[...].reshape(256, 256)
        d_branch = r.d_branch[...].reshape(256, 256)
        hidden = dot(scaled, r.wi[yy], (1, 0)) + r.bias[yy, 0:1, :]
        active, derivative = gelu_parts(hidden)
        active = active.astype(BF16)
        r.branch[...] += dot(active, r.wo[yy], (1, 0))
        r.g_out[dy] = dot(active, d_branch, (0, 0)).astype(BF16)
        d_active = dot(d_branch, r.wo[yy], (1, 1))
        d_hidden = (d_active * derivative).astype(BF16)
        r.g_in[dy] = dot(scaled, d_hidden, (0, 0)).astype(BF16)
        to_core = [
            send(r.g_in.at[dy, :, other_lanes], r.core_in.at[dy], "gc", dy * 2, sibling),
            send(r.g_out.at[dy, other_lanes, :], r.core_out.at[dy], "gc", dy * 2 + 1, sibling),
        ]
        r.d_normed[...] += dot(d_hidden, r.wi[yy], (1, 1))
        return to_core

    def spread(dy, to_core):
        back = (NY - dy) % NY
        to_core[0].wait_recv()
        g_in = r.g_in[dy, :, lanes].astype(F32) + r.core_in[dy].astype(F32)
        r.piece[dy, 0] = g_in[:128].astype(BF16)
        r.piece[dy, 1] = g_in[128:].astype(BF16)
        to_core[1].wait_recv()
        g_out = r.g_out[dy, lanes, :].astype(F32) + r.core_out[dy].astype(F32)
        r.piece[dy, 2] = g_out[:, :128].astype(BF16)
        r.piece[dy, 3] = g_out[:, 128:].astype(BF16)
        for dx in (2, 1, 3, 0):
            if dy or dx:
                index = back * 4 + dx
                send(r.piece.at[dy, (x + dx) % NX], r.piece_in.at[index], "gp", index, plane(back, dx))

    pl.semaphore_wait(relay_2, 5)
    held = None
    for dy in ORDER:
        now = (dy, pair(dy))
        if dy == 1:
            forward_weights(2)
        if held is not None:
            spread(*held)
        held = now

    for s in range(SLOTS):
        d_normed = r.d_normed[s * 64:(s + 1) * 64, :] * r.gain[...]
        normed = r.normed[s].reshape(64, 256)
        mean = jnp.mean(d_normed, axis=-1, keepdims=True)
        along = jnp.mean(d_normed * normed, axis=-1, keepdims=True)
        inverse = r.inverse[s].reshape(64, 128)[:, 0:1]
        d_conv = inverse * (d_normed - mean - normed * along)
        r.d_conv[s] = d_conv.astype(BF16).astype(F32).reshape(TH, TW, 256)
    place(r.grid_d, r.d_conv)
    send_edges(r.grid_d, r.edge_d_out, r.edge_d_in, "ed")
    edges = [send(*copy) for copy in edge_copies(r.edge_d_out, r.edge_d_in, "ed")]
    spread(*held)

    take_edges(r.grid_x, r.edge_x_in)
    for b in range(KS):
        def slot_taps(s, sums):
            sums = list(sums)
            base = r.lats[0, s] * TH
            for i in range(TH + 2 * REACH):
                window = r.grid_x[base + i, LEFT - REACH + b:LEFT - REACH + b + TW, :]
                for a in range(KS):
                    if 0 <= i - a < TH:
                        product = window * r.d_conv[s, i - a]
                        sums[a] += product[:8] + product[8:]
            return tuple(sums)

        sums = lax.fori_loop(
            0, SLOTS, slot_taps, tuple(jnp.zeros((8, 256), F32) for _ in range(KS))
        )
        for a in range(KS):
            line = jnp.sum(sums[a], axis=0, keepdims=True)
            for half in range(2):
                at_row = 2 * (a * KS + b) + half
                owner = at_row // 16
                r.taps[owner % NC, owner // NC, at_row % 16:at_row % 16 + 1, :] = (
                    line[:, half * 128:(half + 1) * 128]
                )
    for at_row in range(2 * KS * KS, 128):
        owner = at_row // 16
        r.taps[owner % NC, owner // NC, at_row % 16:at_row % 16 + 1, :] = jnp.zeros((1, 128), F32)
    k_core = send(r.taps.at[1 - c], r.taps_core, "kc", 0, sibling)
    for s in range(SLOTS):
        r.blocked[s] = (
            (r.cells[s].astype(F32) + r.scale[...] * r.branch[s * 64:(s + 1) * 64, :].reshape(TH, TW, 256))
            * live(s)
        ).astype(BF16)
    give(0)
    k_core.wait_recv()
    r.taps_sum[...] = r.taps[c] + r.taps_core[...]
    spot = y * NX + x
    r.taps_plane[spot] = r.taps_sum[y]
    for step in range(1, 16):
        dy, dx = step // 4, step % 4
        send(r.taps_sum.at[(y + dy) % NY], r.taps_plane.at[spot], "kp", step, plane(dy, dx))

    own = r.piece[0, x].astype(F32)
    for step in range(1, 16):
        remote(
            r.piece.at[0, 0], r.piece_in.at[step], "gp", step, plane(step // 4, step % 4)
        ).wait_recv()
        own += r.piece_in[step].astype(F32)
    r.low_out[...] = own.astype(BF16).reshape(NL, 32, 128)
    for dl in (2, 1, 3):
        send(r.low_out.at[(zl + dl) % NL], r.low_in.at[dl], "gl", dl, low(dl))

    for copy in edges:
        copy.wait_recv()
    take_edges(r.grid_d, r.edge_d_in)

    for step in range(1, 16):
        dy, dx = step // 4, step % 4
        origin = (y + NY - dy) % NY * NX + (x + NX - dx) % NX
        remote(r.taps_sum.at[0], r.taps_plane.at[origin], "kp", step, plane(dy, dx)).wait_recv()
    r.taps_low[zl] = jnp.sum(r.taps_plane[...], axis=0)
    for dl in (2, 1, 3):
        send(r.taps_low.at[zl], r.taps_low.at[zl], "kl", dl, low(dl))

    own = r.low_out[zl].astype(F32)
    for dl in range(1, NL):
        remote(r.low_out.at[0], r.low_in.at[dl], "gl", dl, low(dl)).wait_recv()
        own += r.low_in[dl].astype(F32)
    r.high[zh] = own.astype(BF16)
    for dh in (2, 1, 3):
        send(r.high.at[zh], r.high.at[zh], "gh", dh, high(dh))

    @pl.loop(0, SLOTS)
    def _(s):
        total = depthwise(r.grid_d, s, True)
        for row in range(TH):
            r.cell_grad[s, row] = (
                (r.cot[s, row].astype(F32) + total[row]) * live(s)
            ).astype(BF16)

    give(1)
    for dl in range(1, NL):
        origin = (zl + NL - dl) % NL
        remote(r.taps_low.at[0], r.taps_low.at[origin], "kl", dl, low(dl)).wait_recv()
    r.taps_high[zh] = jnp.sum(r.taps_low[...], axis=0)
    for dh in (2, 1, 3):
        send(r.taps_high.at[zh], r.taps_high.at[zh], "kh", dh, high(dh))

    for dh in range(1, NH):
        origin = (zh + NH - dh) % NH
        remote(r.high.at[0], r.high.at[origin], "gh", dh, high(dh)).wait_recv()
    r.full[x, zl] = (jnp.sum(r.high[...].astype(F32), axis=0) * factor).astype(BF16)
    for step in range(1, 16):
        dl, dx = step // 4, step % 4
        send(r.full.at[x, zl], r.full.at[x, zl], "gg", step, low(dl, dx))

    for dh in range(1, NH):
        origin = (zh + NH - dh) % NH
        remote(r.taps_high.at[0], r.taps_high.at[origin], "kh", dh, high(dh)).wait_recv()
    r.taps_full[m] = jnp.sum(r.taps_high[...], axis=0) * factor
    for index in range(1, 8):
        send(r.taps_full.at[m], r.taps_full.at[m], "km", index, member(index))

    for step in range(1, 16):
        dl, dx = step // 4, step % 4
        remote(
            r.full.at[0, 0],
            r.full.at[(x + NX - dx) % NX, (zl + NL - dl) % NL],
            "gg",
            step,
            low(dl, dx),
        ).wait_recv()
    for half in range(2):
        r.grad_in[half * 128:(half + 1) * 128, :] = r.full[half].reshape(128, 128).astype(F32)
        r.grad_out[:, half * 128:(half + 1) * 128] = (
            r.full[2 + half].reshape(128, 128).astype(F32)
        )
    give(2)
    give(3)
    for index in range(1, 8):
        origin = (y + NY - index // NC) % NY * NC + (c + index) % NC
        remote(r.taps_full.at[0], r.taps_full.at[origin], "km", index, member(index)).wait_recv()
    for a in range(KS):
        for b in range(KS):
            for half in range(2):
                at_row = 2 * (a * KS + b) + half
                r.kernel_grad[a, b:b + 1, half * 128:(half + 1) * 128] = (
                    r.taps_full[at_row // 16, at_row % 16:at_row % 16 + 1, :]
                )
    give(4)
    for copy in sends:
        copy.wait_send()
    for copy in results:
        copy.wait()


def write_kernel(*refs):
    taken = [
        pltpu.make_async_copy(refs[index], refs[10 + index], refs[15].at[index])
        for index in range(5)
    ]
    given = [
        pltpu.make_async_copy(refs[10 + index], refs[5 + index], refs[16].at[index])
        for index in range(5)
    ]
    for copy in taken:
        copy.start()
    for index in range(5):
        taken[index].wait()
        given[index].start()
    for copy in given:
        copy.wait()


def on_device(
    cells, cotangent, slot_lats, slot_count, kernel, ln_gain, w_in, b_in, w_out, layer_scale
):
    cell_count = 8 * 256 * TH * TW
    factor = 1.0 / math.sqrt(cell_count)
    vmem = pl.BlockSpec(memory_space=pltpu.VMEM)
    smem = pl.BlockSpec(memory_space=pltpu.SMEM)
    hbm = pl.BlockSpec(memory_space=pltpu.HBM)
    tiles = jax.ShapeDtypeStruct((SLOTS, TH, TW, 256), BF16)
    shapes = (
        tiles,
        tiles,
        jax.ShapeDtypeStruct((256, 128), F32),
        jax.ShapeDtypeStruct((128, 256), F32),
        jax.ShapeDtypeStruct((KS, KS, 256), F32),
    )
    results = pl.pallas_call(
        functools.partial(block_kernel, factor),
        out_shape=shapes,
        in_specs=[hbm, hbm, smem, smem, hbm, vmem, hbm, vmem, hbm, vmem],
        out_specs=[hbm] * 5,
        scratch_shapes=[pltpu.VMEM(*spec) for spec in VMEM_SCRATCH.values()]
        + [pltpu.SemaphoreType.DMA((n,)) for n in DMA_COUNTS.values() for _ in range(2)]
        + [
            pltpu.SemaphoreType.DMA((len(LOCAL),)),
            pltpu.SemaphoreType.DMA((len(OUTPUTS),)),
            pltpu.SemaphoreType.REGULAR,
            pltpu.SemaphoreType.REGULAR,
        ],
        compiler_params=pltpu.CompilerParams(
            collective_id=0, has_side_effects=True, vmem_limit_bytes=VMEM_BYTES
        ),
        name="block",
    )(
        cells[0],
        cotangent[0],
        slot_lats,
        slot_count,
        kernel,
        ln_gain.reshape(1, 256),
        w_in,
        b_in.reshape(1, 128),
        w_out,
        layer_scale.reshape(1, 256),
    )
    blocked, cell_grad, grad_in, grad_out, kernel_grad = pl.pallas_call(
        write_kernel,
        out_shape=shapes,
        in_specs=[hbm] * 5,
        out_specs=[hbm] * 5,
        scratch_shapes=[pltpu.VMEM(shape.shape, shape.dtype) for shape in shapes]
        + [pltpu.SemaphoreType.DMA((5,)), pltpu.SemaphoreType.DMA((5,))],
        compiler_params=pltpu.CompilerParams(vmem_limit_bytes=VMEM_BYTES),
        name="write",
    )(*results)
    return blocked[None], cell_grad[None], grad_in, grad_out, kernel_grad


def solution(mesh):
    placed = (
        P("member", "tile", None, None, None),
        P("member", "tile", None, None, None),
        P("tile", None),
        P("tile"),
        P(),
        P(),
        P(None, "member"),
        P("member"),
        P("member", None),
        P(),
    )
    return jax.shard_map(
        on_device,
        mesh=mesh,
        in_specs=placed,
        out_specs=(
            P("member", "tile", None, None, None),
            P("member", "tile", None, None, None),
            P(None, "member"),
            P("member", None),
            P(),
        ),
        check_vma=False,
    )
```

```python
import functools
import math

import jax
import jax.numpy as jnp
from jax import lax
from jax.experimental import pallas as pl
from jax.experimental.pallas import tpu as pltpu
from jax.sharding import PartitionSpec as P

NZ, NX, NY, NC = 16, 4, 4, 2
NL, NH = 4, 4
SLOTS, GY, TH, TW, KS = 4, 8, 4, 16, 7
REACH = KS // 2
LEFT = 8
ROWS = GY * TH
EPSILON = 1e-06
MESH = pl.DeviceIdType.MESH
F32, BF16 = jnp.float32, jnp.bfloat16
PEERS = 6 + 2 + 6 + 3 + 1

VMEM_SCRATCH = dict(
    cells=((SLOTS, TH, TW, 256), BF16),
    cot=((SLOTS, TH, TW, 256), BF16),
    kernel=((KS, KS, 256), F32),
    w_in=((256, 128), BF16),
    w_out=((128, 256), BF16),
    blocked=((SLOTS, TH, TW, 256), BF16),
    cell_grad=((SLOTS, TH, TW, 256), BF16),
    strip=((ROWS + 2 * REACH, 16, 256), F32),
    pair_taps=((KS, REACH, 8, 256), F32),
    conv=((SLOTS, TH, TW, 256), F32),
    grid_x=((ROWS + 2 * REACH, 32, 256), F32),
    grid_d=((ROWS + 2 * REACH, 32, 256), F32),
    edge=((2, 96, 256), F32),
    edge_x_out=((2, 96, 256), BF16),
    edge_x_in=((2, 96, 256), BF16),
    edge_d_out=((2, 96, 256), BF16),
    edge_d_in=((2, 96, 256), BF16),
    wi=((NY, 256, 256), BF16),
    wo=((NY, 256, 256), BF16),
    bias_own=((8, 128), F32),
    bias=((NY, 8, 256), F32),
    normed=((SLOTS, TH, TW, 256), F32),
    inverse=((SLOTS, TH, TW, 128), F32),
    scaled=((SLOTS, TH, TW, 256), BF16),
    d_branch=((SLOTS, TH, TW, 256), BF16),
    branch=((256, 256), F32),
    d_normed=((256, 256), F32),
    d_conv=((SLOTS, TH, TW, 256), F32),
    g_in=((NY, 256, 256), BF16),
    g_out=((NY, 256, 256), BF16),
    core_in=((NY, 256, 128), BF16),
    core_out=((NY, 128, 256), BF16),
    piece=((NY, NX, 128, 128), BF16),
    piece_in=((NY * NX, 128, 128), BF16),
    low_out=((NL, 32, 128), BF16),
    low_in=((NL, 32, 128), BF16),
    high=((NH, 32, 128), BF16),
    full_own=((32, 128), BF16),
    taps=((NC, NY, 16, 128), F32),
    taps_core=((NY, 16, 128), F32),
    taps_sum=((NY, 16, 128), F32),
    taps_plane=((NY * NX, 16, 128), F32),
    taps_low=((NL, 16, 128), F32),
    taps_high=((NH, 16, 128), F32),
    taps_own=((16, 128), F32),
)
DMA_COUNTS = dict(
    ex=2, ed=2, wy=9, wc=12, gc=8, gp=16, gl=4, gh=4, gg=16, kc=1, kp=16, kl=4, kh=4, km=8
)
INPUTS = (
    "cells_far", "cot_far", "lats", "count", "kernel_far", "gain", "w_in_far", "b_in", "w_out_far", "scale"
)
LOCAL = ("cells", "w_in", "w_out", "kernel", "cot")
OUTPUTS = ("blocked", "cell_grad", "full", "taps_full")
VMEM_BYTES = 62 * 1024 * 1024


class Refs:
    pass


def gelu_parts(hidden):
    cumulative = 0.5 * (1.0 + lax.erf(hidden * 0.7071067811865476))
    density = jnp.exp(-0.5 * hidden * hidden) * 0.3989422804014327
    return (hidden * cumulative, cumulative + hidden * density)


def dot(a, b, contract):
    return lax.dot_general(a, b, ((contract[0:1], contract[1:2]), ((), ())), preferred_element_type=F32)


def block_kernel(factor, *refs):
    r = Refs()
    names = INPUTS + tuple(name + "_far" for name in OUTPUTS) + tuple(VMEM_SCRATCH)
    for name, ref in zip(names, refs):
        setattr(r, name, ref)
    sems = {}
    rest = refs[len(names):]
    for index, name in enumerate(DMA_COUNTS):
        sems[name] = (rest[2 * index], rest[2 * index + 1])
    local_sems, result_sems, relay_1, relay_2 = rest[2 * len(DMA_COUNTS):]
    local = {}
    for index, name in enumerate(LOCAL):
        local[name] = pltpu.make_async_copy(
            getattr(r, name + "_far"), getattr(r, name), local_sems.at[index]
        )
        local[name].start()
    results = []

    def give(index, source, target):
        copy = pltpu.make_async_copy(source, target, result_sems.at[index])
        copy.start()
        results.append(copy)


    t, m = lax.axis_index("tile"), lax.axis_index("member")
    z, x, y, c = t // NX, t % NX, m // NC, m % NC
    zh, zl = z // NL, z % NL
    sends = []

    def at(zz, xx, yy, cc):
        return {"tile": zz * NX + xx, "member": yy * NC + cc}

    def plane(dy, dx):
        return at(z, (x + dx) % NX, (y + dy) % NY, c)

    def low(dl, dx=0):
        return at(zh * NL + (zl + dl) % NL, (x + dx) % NX, y, c)

    def high(dh):
        return at((zh + dh) % NH * NL + zl, x, y, c)

    def member(index):
        return at(z, x, (y + index // NC) % NY, (c + index) % NC)

    def remote(src, dst, name, index, target):
        return pltpu.make_async_remote_copy(
            src_ref=src,
            dst_ref=dst,
            send_sem=sems[name][0].at[index],
            recv_sem=sems[name][1].at[index],
            device_id=target,
            device_id_type=MESH,
        )

    def send(*copy):
        made = remote(*copy)
        made.start()
        sends.append(made)
        return made

    left = {"tile": (t + NZ * NX - 1) % (NZ * NX), "member": m}
    right = {"tile": (t + 1) % (NZ * NX), "member": m}
    sibling = at(z, x, y, 1 - c)

    barrier = pltpu.get_barrier_semaphore()

    def greet(target):
        pl.semaphore_signal(barrier, inc=1, device_id=target, device_id_type=MESH)

    def along(dz):
        return at((z + NZ + dz) % NZ, x, y, c)

    for dz in (3, -3, 2, -2, 1, -1):
        greet(along(dz))
    greet(left)
    greet(right)
    for dy in range(1, NY):
        greet(plane(dy, 0))
        greet(at(z, x, (y + dy) % NY, 1 - c))
    for dx in range(1, NX):
        greet(plane(0, dx))
    greet(sibling)

    def relay(semaphore, targets):
        for target in targets:
            pl.semaphore_signal(semaphore, inc=1, device_id=target, device_id_type=MESH)

    def live(s):
        return jnp.where(s < r.count[0], 1.0, 0.0).astype(F32)

    def place(grid, values):
        grid[...] = jnp.zeros_like(grid)

        @pl.loop(0, GY)
        def _(g):
            found, weight = jnp.int32(0), jnp.float32(0.0)
            for s in range(SLOTS):
                hit = jnp.where(r.lats[0, s] == g, 1, 0)
                found += hit * s
                weight += hit.astype(F32) * live(s)
            tile = values[jnp.minimum(found, SLOTS - 1)].astype(F32) * weight
            grid[pl.ds(REACH + g * TH, TH), LEFT:LEFT + TW, :] = tile

    def send_edges(grid, out, landing, name):
        for row in range(ROWS):
            spot = slice(3 * row, 3 * row + 3)
            r.edge[0, spot, :] = grid[REACH + row, LEFT:LEFT + 3, :]
            r.edge[1, spot, :] = grid[REACH + row, LEFT + TW - 3:LEFT + TW, :]
        out[...] = r.edge[...].astype(BF16)

    def edge_copies(out, landing, name):
        return (
            (out.at[0], landing.at[1], name, 0, left),
            (out.at[1], landing.at[0], name, 1, right),
        )

    def take_edges(grid, landing):
        r.edge[...] = landing[...].astype(F32)
        for row in range(ROWS):
            spot = slice(3 * row, 3 * row + 3)
            grid[REACH + row, LEFT - 3:LEFT, :] = r.edge[0, spot, :]
            grid[REACH + row, LEFT + TW:LEFT + TW + 3, :] = r.edge[1, spot, :]

    def depthwise(grid, s, flipped):
        base = r.lats[0, s] * TH
        total = [jnp.zeros((TW, 256), F32) for _ in range(TH)]
        for b in range(KS):
            for i in range(TH + 2 * REACH):
                window = grid[base + i, LEFT - REACH + b:LEFT - REACH + b + TW, :]
                for a in range(KS):
                    if 0 <= i - a < TH:
                        ka, kb = (KS - 1 - a, KS - 1 - b) if flipped else (a, b)
                        total[i - a] += window * r.kernel[ka, kb:kb + 1, :]
        return total

    r.bias_own[...] = jnp.broadcast_to(r.b_in[...].astype(F32), (8, 128))
    lanes = pl.ds(pl.multiple_of(c * 128, 128), 128)
    other_lanes = pl.ds(pl.multiple_of((1 - c) * 128, 128), 128)
    r.bias[y, :, lanes] = r.bias_own[...]
    local["cells"].wait()
    place(r.grid_x, r.cells)
    send_edges(r.grid_x, r.edge_x_out, r.edge_x_in, "ex")

    local["w_in"].wait()
    local["w_out"].wait()
    r.wi[y, :, lanes] = r.w_in[...]
    r.wo[y, lanes, :] = r.w_out[...]
    pl.semaphore_wait(barrier, PEERS)
    relay(
        relay_1,
        [plane(dy, 0) for dy in range(1, NY)]
        + [plane(0, dx) for dx in range(1, NX)]
        + [along(2), along(-2)],
    )

    edges = [send(*copy) for copy in edge_copies(r.edge_x_out, r.edge_x_in, "ex")]

    def weights(yy):
        return (
            r.wi.at[yy, :, lanes],
            r.wo.at[yy, lanes, :],
            r.bias.at[yy, :, lanes],
        )

    def weights_other(yy):
        return (
            r.wi.at[yy, :, other_lanes],
            r.wo.at[yy, other_lanes, :],
            r.bias.at[yy, :, other_lanes],
        )

    for dy in (1, 3, 2):
        for kind, part in enumerate(weights(y)):
            send(part, part, "wy", (dy - 1) * 3 + kind, plane(dy, 0))
    for kind, part in enumerate(weights(y)):
        send(part, part, "wc", kind, sibling)

    def forward_weights(dy):
        yy = (y + NY - dy) % NY
        for kind, part in enumerate(weights(yy)):
            remote(part, part, "wy", (dy - 1) * 3 + kind, plane(dy, 0)).wait_recv()
            send(part, part, "wc", dy * 3 + kind, sibling)

    local["kernel"].wait()
    low_half = lax.broadcasted_iota(jnp.int32, (8, 256), 0) < 4
    for a in range(KS):
        for b in range(REACH):
            r.pair_taps[a, b] = jnp.where(
                low_half, r.kernel[a, b:b + 1, :], r.kernel[a, b + 4:b + 5, :]
            )

    @pl.loop(0, SLOTS)
    def _(s):
        total = depthwise(r.grid_x, s, False)
        for row in range(TH):
            r.conv[s, row] = total[row]

    r.strip[...] = jnp.zeros_like(r.strip)
    local["cot"].wait()
    for s in range(SLOTS):
        r.d_branch[s] = (
            r.cot[s].astype(F32) * (r.scale[...] * live(s))
        ).astype(BF16)
    r.branch[...] = jnp.zeros_like(r.branch)
    r.d_normed[...] = jnp.zeros_like(r.d_normed)

    pl.semaphore_wait(relay_1, 8)
    relay(
        relay_2, [plane(0, dx) for dx in range(1, NX)] + [along(4), along(-4)]
    )
    for copy in edges:
        copy.wait_recv()
    r.edge[...] = r.edge_x_in[...].astype(F32)
    for row in range(ROWS):
        spot = slice(3 * row, 3 * row + 3)
        r.strip[REACH + row, 0:3, :] = r.edge[0, spot, :]
        r.strip[REACH + row, 7:10, :] = r.edge[1, spot, :]

    @pl.loop(0, SLOTS)
    def _(s):
        base = r.lats[0, s] * TH
        outer = [jnp.zeros((8, 256), F32) for _ in range(TH)]
        for b in range(REACH):
            for i in range(TH + 2 * REACH):
                window = r.strip[base + i, b:b + 8, :]
                for a in range(KS):
                    if 0 <= i - a < TH:
                        outer[i - a] += window * r.pair_taps[a, b]
        for row in range(TH):
            total = r.conv[s, row] + jnp.concatenate(
                [jnp.where(low_half, outer[row], 0.0), jnp.where(low_half, 0.0, outer[row])], axis=0
            )
            center = total - jnp.mean(total, axis=-1, keepdims=True)
            inverse = lax.rsqrt(jnp.mean(center * center, axis=-1, keepdims=True) + EPSILON)
            normed = center * inverse
            r.normed[s, row] = normed
            r.inverse[s, row] = jnp.broadcast_to(inverse, (TW, 128))
            r.scaled[s, row] = (normed * r.gain[...]).astype(BF16)

    def pair(dy):
        yy = (y + NY - dy) % NY
        for kind, part in enumerate(weights_other(yy)):
            remote(part, part, "wc", dy * 3 + kind, sibling).wait_recv()
        scaled = r.scaled[...].reshape(256, 256)
        d_branch = r.d_branch[...].reshape(256, 256)
        hidden = dot(scaled, r.wi[yy], (1, 0)) + r.bias[yy, 0:1, :]
        active, derivative = gelu_parts(hidden)
        active = active.astype(BF16)
        r.branch[...] += dot(active, r.wo[yy], (1, 0))
        r.g_out[dy] = dot(active, d_branch, (0, 0)).astype(BF16)
        d_active = dot(d_branch, r.wo[yy], (1, 1))
        d_hidden = (d_active * derivative).astype(BF16)
        r.g_in[dy] = dot(scaled, d_hidden, (0, 0)).astype(BF16)
        to_core = [
            send(r.g_in.at[dy, :, other_lanes], r.core_in.at[dy], "gc", dy * 2, sibling),
            send(r.g_out.at[dy, other_lanes, :], r.core_out.at[dy], "gc", dy * 2 + 1, sibling),
        ]
        r.d_normed[...] += dot(d_hidden, r.wi[yy], (1, 1))
        return to_core

    def spread(dy, to_core):
        back = (NY - dy) % NY
        to_core[0].wait_recv()
        g_in = r.g_in[dy, :, lanes].astype(F32) + r.core_in[dy].astype(F32)
        r.piece[dy, 0] = g_in[:128].astype(BF16)
        r.piece[dy, 1] = g_in[128:].astype(BF16)
        to_core[1].wait_recv()
        g_out = r.g_out[dy, lanes, :].astype(F32) + r.core_out[dy].astype(F32)
        r.piece[dy, 2] = g_out[:, :128].astype(BF16)
        r.piece[dy, 3] = g_out[:, 128:].astype(BF16)
        for dx in (2, 1, 3, 0):
            if dy or dx:
                index = back * 4 + dx
                send(r.piece.at[dy, (x + dx) % NX], r.piece_in.at[index], "gp", index, plane(back, dx))

    forward_weights(1)
    forward_weights(3)
    pl.semaphore_wait(relay_2, 5)
    first = pair(1)
    second = pair(3)
    spread(1, first)
    own_pair = pair(0)
    spread(3, second)
    forward_weights(2)
    spread(0, own_pair)
    last = pair(2)

    for s in range(SLOTS):
        d_normed = r.d_normed[s * 64:(s + 1) * 64, :] * r.gain[...]
        normed = r.normed[s].reshape(64, 256)
        mean = jnp.mean(d_normed, axis=-1, keepdims=True)
        along = jnp.mean(d_normed * normed, axis=-1, keepdims=True)
        inverse = r.inverse[s].reshape(64, 128)[:, 0:1]
        d_conv = inverse * (d_normed - mean - normed * along)
        r.d_conv[s] = d_conv.astype(BF16).astype(F32).reshape(TH, TW, 256)
    place(r.grid_d, r.d_conv)
    send_edges(r.grid_d, r.edge_d_out, r.edge_d_in, "ed")
    edges = [send(*copy) for copy in edge_copies(r.edge_d_out, r.edge_d_in, "ed")]
    spread(2, last)

    take_edges(r.grid_x, r.edge_x_in)
    for b in range(KS):
        def slot_taps(s, sums):
            sums = list(sums)
            base = r.lats[0, s] * TH
            for i in range(TH + 2 * REACH):
                window = r.grid_x[base + i, LEFT - REACH + b:LEFT - REACH + b + TW, :]
                for a in range(KS):
                    if 0 <= i - a < TH:
                        product = window * r.d_conv[s, i - a]
                        sums[a] += product[:8] + product[8:]
            return tuple(sums)

        sums = lax.fori_loop(
            0, SLOTS, slot_taps, tuple(jnp.zeros((8, 256), F32) for _ in range(KS))
        )
        for a in range(KS):
            line = jnp.sum(sums[a], axis=0, keepdims=True)
            for half in range(2):
                at_row = 2 * (a * KS + b) + half
                owner = at_row // 16
                r.taps[owner % NC, owner // NC, at_row % 16:at_row % 16 + 1, :] = (
                    line[:, half * 128:(half + 1) * 128]
                )
    for at_row in range(2 * KS * KS, 128):
        owner = at_row // 16
        r.taps[owner % NC, owner // NC, at_row % 16:at_row % 16 + 1, :] = jnp.zeros((1, 128), F32)
    k_core = send(r.taps.at[1 - c], r.taps_core, "kc", 0, sibling)
    for s in range(SLOTS):
        r.blocked[s] = (
            (r.cells[s].astype(F32) + r.scale[...] * r.branch[s * 64:(s + 1) * 64, :].reshape(TH, TW, 256))
            * live(s)
        ).astype(BF16)
    give(0, r.blocked, r.blocked_far)
    k_core.wait_recv()
    r.taps_sum[...] = r.taps[c] + r.taps_core[...]
    spot = y * NX + x
    r.taps_plane[spot] = r.taps_sum[y]
    for step in range(1, 16):
        dy, dx = step // 4, step % 4
        send(r.taps_sum.at[(y + dy) % NY], r.taps_plane.at[spot], "kp", step, plane(dy, dx))

    own = r.piece[0, x].astype(F32)
    for step in range(1, 16):
        remote(
            r.piece.at[0, 0], r.piece_in.at[step], "gp", step, plane(step // 4, step % 4)
        ).wait_recv()
        own += r.piece_in[step].astype(F32)
    r.low_out[...] = own.astype(BF16).reshape(NL, 32, 128)
    for dl in (2, 1, 3):
        send(r.low_out.at[(zl + dl) % NL], r.low_in.at[dl], "gl", dl, low(dl))

    for copy in edges:
        copy.wait_recv()
    take_edges(r.grid_d, r.edge_d_in)

    for step in range(1, 16):
        dy, dx = step // 4, step % 4
        origin = (y + NY - dy) % NY * NX + (x + NX - dx) % NX
        remote(r.taps_sum.at[0], r.taps_plane.at[origin], "kp", step, plane(dy, dx)).wait_recv()
    r.taps_low[zl] = jnp.sum(r.taps_plane[...], axis=0)
    for dl in (2, 1, 3):
        send(r.taps_low.at[zl], r.taps_low.at[zl], "kl", dl, low(dl))

    own = r.low_out[zl].astype(F32)
    for dl in range(1, NL):
        remote(r.low_out.at[0], r.low_in.at[dl], "gl", dl, low(dl)).wait_recv()
        own += r.low_in[dl].astype(F32)
    r.high[zh] = own.astype(BF16)
    for dh in (2, 1, 3):
        send(r.high.at[zh], r.high.at[zh], "gh", dh, high(dh))

    for dl in range(1, NL):
        origin = (zl + NL - dl) % NL
        remote(r.taps_low.at[0], r.taps_low.at[origin], "kl", dl, low(dl)).wait_recv()
    r.taps_high[zh] = jnp.sum(r.taps_low[...], axis=0)
    for dh in (2, 1, 3):
        send(r.taps_high.at[zh], r.taps_high.at[zh], "kh", dh, high(dh))

    @pl.loop(0, SLOTS)
    def _(s):
        total = depthwise(r.grid_d, s, True)
        for row in range(TH):
            r.cell_grad[s, row] = (
                (r.cot[s, row].astype(F32) + total[row]) * live(s)
            ).astype(BF16)

    give(1, r.cell_grad, r.cell_grad_far)


    for dh in range(1, NH):
        origin = (zh + NH - dh) % NH
        remote(r.high.at[0], r.high.at[origin], "gh", dh, high(dh)).wait_recv()
    r.full_own[...] = (jnp.sum(r.high[...].astype(F32), axis=0) * factor).astype(BF16)
    for step in range(1, 16):
        dl, dx = step // 4, step % 4
        send(r.full_own, r.full_far.at[x, zl], "gg", step, low(dl, dx))
    give(2, r.full_own, r.full_far.at[x, zl])

    for dh in range(1, NH):
        origin = (zh + NH - dh) % NH
        remote(r.taps_high.at[0], r.taps_high.at[origin], "kh", dh, high(dh)).wait_recv()
    r.taps_own[...] = jnp.sum(r.taps_high[...], axis=0) * factor
    for index in range(1, 8):
        send(r.taps_own, r.taps_full_far.at[m], "km", index, member(index))
    give(3, r.taps_own, r.taps_full_far.at[m])

    for step in range(1, 16):
        dl, dx = step // 4, step % 4
        remote(
            r.full_own,
            r.full_far.at[(x + NX - dx) % NX, (zl + NL - dl) % NL],
            "gg",
            step,
            low(dl, dx),
        ).wait_recv()
    for index in range(1, 8):
        origin = (y + NY - index // NC) % NY * NC + (c + index) % NC
        remote(r.taps_own, r.taps_full_far.at[origin], "km", index, member(index)).wait_recv()
    for copy in sends:
        copy.wait_send()
    for copy in results:
        copy.wait()


def write_kernel(*refs):
    far, out, near = refs[:4], refs[4:9], refs[9:16]
    blocked, cell_grad, full, taps, grad_in, grad_out, kernel_grad = near
    take_sems, give_sems = refs[16:]
    taken = [
        pltpu.make_async_copy(far[index], near[index], take_sems.at[index]) for index in range(4)
    ]
    given = [
        pltpu.make_async_copy(source, out[index], give_sems.at[index])
        for index, source in enumerate((blocked, cell_grad, grad_in, grad_out, kernel_grad))
    ]
    for index in (2, 3, 0, 1):
        taken[index].start()
    taken[2].wait()
    for half in range(2):
        part = slice(half * 128, (half + 1) * 128)
        grad_in[part, :] = full[half].reshape(128, 128).astype(F32)
        grad_out[:, part] = full[2 + half].reshape(128, 128).astype(F32)
    given[2].start()
    given[3].start()
    taken[0].wait()
    given[0].start()
    taken[1].wait()
    given[1].start()
    taken[3].wait()
    for a in range(KS):
        for b in range(KS):
            for half in range(2):
                at_row = 2 * (a * KS + b) + half
                kernel_grad[a, b:b + 1, half * 128:(half + 1) * 128] = (
                    taps[at_row // 16, at_row % 16:at_row % 16 + 1, :]
                )
    given[4].start()
    for copy in given:
        copy.wait()


def on_device(
    cells, cotangent, slot_lats, slot_count, kernel, ln_gain, w_in, b_in, w_out, layer_scale
):
    cell_count = 8 * 256 * TH * TW
    factor = 1.0 / math.sqrt(cell_count)
    vmem = pl.BlockSpec(memory_space=pltpu.VMEM)
    smem = pl.BlockSpec(memory_space=pltpu.SMEM)
    hbm = pl.BlockSpec(memory_space=pltpu.HBM)
    tiles = jax.ShapeDtypeStruct((SLOTS, TH, TW, 256), BF16)
    shapes = (
        tiles,
        tiles,
        jax.ShapeDtypeStruct((256, 128), F32),
        jax.ShapeDtypeStruct((128, 256), F32),
        jax.ShapeDtypeStruct((KS, KS, 256), F32),
    )
    parts = (
        tiles,
        tiles,
        jax.ShapeDtypeStruct((NX, NL, 32, 128), BF16),
        jax.ShapeDtypeStruct((NY * NC, 16, 128), F32),
    )
    results = pl.pallas_call(
        functools.partial(block_kernel, factor),
        out_shape=parts,
        in_specs=[hbm, hbm, smem, smem, hbm, vmem, hbm, vmem, hbm, vmem],
        out_specs=[hbm] * 4,
        scratch_shapes=[pltpu.VMEM(*spec) for spec in VMEM_SCRATCH.values()]
        + [pltpu.SemaphoreType.DMA((n,)) for n in DMA_COUNTS.values() for _ in range(2)]
        + [
            pltpu.SemaphoreType.DMA((len(LOCAL),)),
            pltpu.SemaphoreType.DMA((len(OUTPUTS),)),
            pltpu.SemaphoreType.REGULAR,
            pltpu.SemaphoreType.REGULAR,
        ],
        compiler_params=pltpu.CompilerParams(
            collective_id=0, has_side_effects=True, vmem_limit_bytes=VMEM_BYTES
        ),
        name="block",
    )(
        cells[0],
        cotangent[0],
        slot_lats,
        slot_count,
        kernel,
        ln_gain.reshape(1, 256),
        w_in,
        b_in.reshape(1, 128),
        w_out,
        layer_scale.reshape(1, 256),
    )
    blocked, cell_grad, grad_in, grad_out, kernel_grad = pl.pallas_call(
        write_kernel,
        out_shape=shapes,
        in_specs=[hbm] * 4,
        out_specs=[hbm] * 5,
        scratch_shapes=[pltpu.VMEM(shape.shape, shape.dtype) for shape in parts + shapes[2:]]
        + [pltpu.SemaphoreType.DMA((4,)), pltpu.SemaphoreType.DMA((5,))],
        compiler_params=pltpu.CompilerParams(vmem_limit_bytes=VMEM_BYTES),
        name="write",
    )(*results)
    return blocked[None], cell_grad[None], grad_in, grad_out, kernel_grad


def solution(mesh):
    placed = (
        P("member", "tile", None, None, None),
        P("member", "tile", None, None, None),
        P("tile", None),
        P("tile"),
        P(),
        P(),
        P(None, "member"),
        P("member"),
        P("member", None),
        P(),
    )
    return jax.shard_map(
        on_device,
        mesh=mesh,
        in_specs=placed,
        out_specs=(
            P("member", "tile", None, None, None),
            P("member", "tile", None, None, None),
            P(None, "member"),
            P("member", None),
            P(),
        ),
        check_vma=False,
    )
```

```python
import functools
import math

import jax
import jax.numpy as jnp
from jax import lax
from jax.experimental import pallas as pl
from jax.experimental.pallas import tpu as pltpu
from jax.sharding import PartitionSpec as P

NZ, NX, NY, NC = 16, 4, 4, 2
NL, NH = 4, 4
SLOTS, GY, TH, TW, KS = 4, 8, 4, 16, 7
REACH = KS // 2
LEFT = 8
ROWS = GY * TH
EPSILON = 1e-06
MESH = pl.DeviceIdType.MESH
F32, BF16 = jnp.float32, jnp.bfloat16
PEERS = 6 + 2 + 6 + 3 + 1

VMEM_SCRATCH = dict(
    cells=((SLOTS, TH, TW, 256), BF16),
    cot=((SLOTS, TH, TW, 256), BF16),
    kernel=((KS, KS, 256), F32),
    w_in=((256, 128), BF16),
    w_out=((128, 256), BF16),
    blocked=((SLOTS, TH, TW, 256), BF16),
    cell_grad=((SLOTS, TH, TW, 256), BF16),
    strip=((ROWS + 2 * REACH, 16, 256), F32),
    pair_taps=((KS, REACH, 8, 256), F32),
    conv=((SLOTS, TH, TW, 256), F32),
    grid_x=((ROWS + 2 * REACH, 32, 256), F32),
    grid_d=((ROWS + 2 * REACH, 32, 256), F32),
    edge=((2, 96, 256), F32),
    edge_x_out=((2, 96, 256), BF16),
    edge_x_in=((2, 96, 256), BF16),
    edge_d_out=((2, 96, 256), BF16),
    edge_d_in=((2, 96, 256), BF16),
    wi=((NY, 256, 256), BF16),
    wo=((NY, 256, 256), BF16),
    bias_own=((8, 128), F32),
    bias=((NY, 8, 256), F32),
    normed=((SLOTS, TH, TW, 256), F32),
    inverse=((SLOTS, TH, TW, 128), F32),
    scaled=((SLOTS, TH, TW, 256), BF16),
    d_branch=((SLOTS, TH, TW, 256), BF16),
    branch=((256, 256), F32),
    d_normed=((256, 256), F32),
    d_conv=((SLOTS, TH, TW, 256), F32),
    g_in=((NY, 256, 256), BF16),
    g_out=((NY, 256, 256), BF16),
    core_in=((NY, 256, 128), BF16),
    core_out=((NY, 128, 256), BF16),
    piece=((NY, NX, 128, 128), BF16),
    piece_in=((NY * NX, 128, 128), BF16),
    low_out=((NL, 32, 128), BF16),
    low_in=((NL, 32, 128), BF16),
    high=((NH, 32, 128), BF16),
    full_own=((32, 128), BF16),
    taps=((NC, NY, 16, 128), F32),
    taps_core=((NY, 16, 128), F32),
    taps_sum=((NY, 16, 128), F32),
    taps_plane=((NY * NX, 16, 128), F32),
    taps_low=((NL, 16, 128), F32),
    taps_high=((NH, 16, 128), F32),
    taps_own=((16, 128), F32),
)
DMA_COUNTS = dict(
    ex=2, ed=2, wy=9, wc=12, gc=8, gp=16, gl=4, gh=4, gg=16, kc=1, kp=16, kl=4, kh=4, km=8
)
INPUTS = (
    "cells_far", "cot_far", "lats", "count", "kernel_far", "gain", "w_in_far", "b_in", "w_out_far", "scale"
)
LOCAL = ("cells", "w_in", "w_out", "kernel", "cot")
OUTPUTS = ("blocked", "cell_grad", "full", "taps_full")
VMEM_BYTES = 62 * 1024 * 1024


class Refs:
    pass


def gelu_parts(hidden):
    cumulative = 0.5 * (1.0 + lax.erf(hidden * 0.7071067811865476))
    density = jnp.exp(-0.5 * hidden * hidden) * 0.3989422804014327
    return (hidden * cumulative, cumulative + hidden * density)


def dot(a, b, contract):
    return lax.dot_general(a, b, ((contract[0:1], contract[1:2]), ((), ())), preferred_element_type=F32)


def block_kernel(factor, *refs):
    r = Refs()
    names = INPUTS + tuple(name + "_far" for name in OUTPUTS) + tuple(VMEM_SCRATCH)
    for name, ref in zip(names, refs):
        setattr(r, name, ref)
    sems = {}
    rest = refs[len(names):]
    for index, name in enumerate(DMA_COUNTS):
        sems[name] = (rest[2 * index], rest[2 * index + 1])
    local_sems, result_sems, relay_1, relay_2 = rest[2 * len(DMA_COUNTS):]
    local = {}
    for index, name in enumerate(LOCAL):
        local[name] = pltpu.make_async_copy(
            getattr(r, name + "_far"), getattr(r, name), local_sems.at[index]
        )
        local[name].start()
    results = []

    def give(index, source, target):
        copy = pltpu.make_async_copy(source, target, result_sems.at[index])
        copy.start()
        results.append(copy)


    t, m = lax.axis_index("tile"), lax.axis_index("member")
    z, x, y, c = t // NX, t % NX, m // NC, m % NC
    zh, zl = z // NL, z % NL
    sends = []

    def at(zz, xx, yy, cc):
        return {"tile": zz * NX + xx, "member": yy * NC + cc}

    def plane(dy, dx):
        return at(z, (x + dx) % NX, (y + dy) % NY, c)

    def low(dl, dx=0):
        return at(zh * NL + (zl + dl) % NL, (x + dx) % NX, y, c)

    def high(dh):
        return at((zh + dh) % NH * NL + zl, x, y, c)

    def member(index):
        return at(z, x, (y + index // NC) % NY, (c + index) % NC)

    def remote(src, dst, name, index, target):
        return pltpu.make_async_remote_copy(
            src_ref=src,
            dst_ref=dst,
            send_sem=sems[name][0].at[index],
            recv_sem=sems[name][1].at[index],
            device_id=target,
            device_id_type=MESH,
        )

    def send(*copy):
        made = remote(*copy)
        made.start()
        sends.append(made)
        return made

    left = {"tile": (t + NZ * NX - 1) % (NZ * NX), "member": m}
    right = {"tile": (t + 1) % (NZ * NX), "member": m}
    sibling = at(z, x, y, 1 - c)

    barrier = pltpu.get_barrier_semaphore()

    def greet(target):
        pl.semaphore_signal(barrier, inc=1, device_id=target, device_id_type=MESH)

    def along(dz):
        return at((z + NZ + dz) % NZ, x, y, c)

    for dz in (3, -3, 2, -2, 1, -1):
        greet(along(dz))
    greet(left)
    greet(right)
    for dy in range(1, NY):
        greet(plane(dy, 0))
        greet(at(z, x, (y + dy) % NY, 1 - c))
    for dx in range(1, NX):
        greet(plane(0, dx))
    greet(sibling)

    def relay(semaphore, targets):
        for target in targets:
            pl.semaphore_signal(semaphore, inc=1, device_id=target, device_id_type=MESH)

    def live(s):
        return jnp.where(s < r.count[0], 1.0, 0.0).astype(F32)

    def place(grid, values):
        grid[...] = jnp.zeros_like(grid)

        @pl.loop(0, GY)
        def _(g):
            found, weight = jnp.int32(0), jnp.float32(0.0)
            for s in range(SLOTS):
                hit = jnp.where(r.lats[0, s] == g, 1, 0)
                found += hit * s
                weight += hit.astype(F32) * live(s)
            tile = values[jnp.minimum(found, SLOTS - 1)].astype(F32) * weight
            grid[pl.ds(REACH + g * TH, TH), LEFT:LEFT + TW, :] = tile

    def send_edges(grid, out, landing, name):
        for row in range(ROWS):
            spot = slice(3 * row, 3 * row + 3)
            r.edge[0, spot, :] = grid[REACH + row, LEFT:LEFT + 3, :]
            r.edge[1, spot, :] = grid[REACH + row, LEFT + TW - 3:LEFT + TW, :]
        out[...] = r.edge[...].astype(BF16)

    def edge_copies(out, landing, name):
        return (
            (out.at[0], landing.at[1], name, 0, left),
            (out.at[1], landing.at[0], name, 1, right),
        )

    def take_edges(grid, landing):
        r.edge[...] = landing[...].astype(F32)
        for row in range(ROWS):
            spot = slice(3 * row, 3 * row + 3)
            grid[REACH + row, LEFT - 3:LEFT, :] = r.edge[0, spot, :]
            grid[REACH + row, LEFT + TW:LEFT + TW + 3, :] = r.edge[1, spot, :]

    def depthwise(grid, s, flipped):
        base = r.lats[0, s] * TH
        total = [jnp.zeros((TW, 256), F32) for _ in range(TH)]
        for b in range(KS):
            for i in range(TH + 2 * REACH):
                window = grid[base + i, LEFT - REACH + b:LEFT - REACH + b + TW, :]
                for a in range(KS):
                    if 0 <= i - a < TH:
                        ka, kb = (KS - 1 - a, KS - 1 - b) if flipped else (a, b)
                        total[i - a] += window * r.kernel[ka, kb:kb + 1, :]
        return total

    r.bias_own[...] = jnp.broadcast_to(r.b_in[...].astype(F32), (8, 128))
    lanes = pl.ds(pl.multiple_of(c * 128, 128), 128)
    other_lanes = pl.ds(pl.multiple_of((1 - c) * 128, 128), 128)
    r.bias[y, :, lanes] = r.bias_own[...]
    local["cells"].wait()
    place(r.grid_x, r.cells)
    send_edges(r.grid_x, r.edge_x_out, r.edge_x_in, "ex")

    local["w_in"].wait()
    local["w_out"].wait()
    r.wi[y, :, lanes] = r.w_in[...]
    r.wo[y, lanes, :] = r.w_out[...]
    pl.semaphore_wait(barrier, PEERS)
    relay(
        relay_1,
        [plane(dy, 0) for dy in range(1, NY)]
        + [plane(0, dx) for dx in range(1, NX)]
        + [along(2), along(-2)],
    )

    edges = [send(*copy) for copy in edge_copies(r.edge_x_out, r.edge_x_in, "ex")]

    def weights(yy):
        return (
            r.wi.at[yy, :, lanes],
            r.wo.at[yy, lanes, :],
            r.bias.at[yy, :, lanes],
        )

    def weights_other(yy):
        return (
            r.wi.at[yy, :, other_lanes],
            r.wo.at[yy, other_lanes, :],
            r.bias.at[yy, :, other_lanes],
        )

    for dy in (1, 3, 2):
        for kind, part in enumerate(weights(y)):
            send(part, part, "wy", (dy - 1) * 3 + kind, plane(dy, 0))
    for kind, part in enumerate(weights(y)):
        send(part, part, "wc", kind, sibling)

    def forward_weights(dy):
        yy = (y + NY - dy) % NY
        for kind, part in enumerate(weights(yy)):
            remote(part, part, "wy", (dy - 1) * 3 + kind, plane(dy, 0)).wait_recv()
            send(part, part, "wc", dy * 3 + kind, sibling)

    local["kernel"].wait()
    low_half = lax.broadcasted_iota(jnp.int32, (8, 256), 0) < 4
    for a in range(KS):
        for b in range(REACH):
            r.pair_taps[a, b] = jnp.where(
                low_half, r.kernel[a, b:b + 1, :], r.kernel[a, b + 4:b + 5, :]
            )

    @pl.loop(0, SLOTS)
    def _(s):
        total = depthwise(r.grid_x, s, False)
        for row in range(TH):
            r.conv[s, row] = total[row]

    r.strip[...] = jnp.zeros_like(r.strip)
    local["cot"].wait()
    for s in range(SLOTS):
        r.d_branch[s] = (
            r.cot[s].astype(F32) * (r.scale[...] * live(s))
        ).astype(BF16)
    r.branch[...] = jnp.zeros_like(r.branch)
    r.d_normed[...] = jnp.zeros_like(r.d_normed)

    pl.semaphore_wait(relay_1, 8)
    relay(
        relay_2, [plane(0, dx) for dx in range(1, NX)] + [along(4), along(-4)]
    )
    for copy in edges:
        copy.wait_recv()
    r.edge[...] = r.edge_x_in[...].astype(F32)
    for row in range(ROWS):
        spot = slice(3 * row, 3 * row + 3)
        r.strip[REACH + row, 0:3, :] = r.edge[0, spot, :]
        r.strip[REACH + row, 7:10, :] = r.edge[1, spot, :]

    @pl.loop(0, SLOTS)
    def _(s):
        base = r.lats[0, s] * TH
        outer = [jnp.zeros((8, 256), F32) for _ in range(TH)]
        for b in range(REACH):
            for i in range(TH + 2 * REACH):
                window = r.strip[base + i, b:b + 8, :]
                for a in range(KS):
                    if 0 <= i - a < TH:
                        outer[i - a] += window * r.pair_taps[a, b]
        for row in range(TH):
            total = r.conv[s, row] + jnp.concatenate(
                [jnp.where(low_half, outer[row], 0.0), jnp.where(low_half, 0.0, outer[row])], axis=0
            )
            center = total - jnp.mean(total, axis=-1, keepdims=True)
            inverse = lax.rsqrt(jnp.mean(center * center, axis=-1, keepdims=True) + EPSILON)
            normed = center * inverse
            r.normed[s, row] = normed
            r.inverse[s, row] = jnp.broadcast_to(inverse, (TW, 128))
            r.scaled[s, row] = (normed * r.gain[...]).astype(BF16)

    def pair(dy):
        yy = (y + NY - dy) % NY
        for kind, part in enumerate(weights_other(yy)):
            remote(part, part, "wc", dy * 3 + kind, sibling).wait_recv()
        scaled = r.scaled[...].reshape(256, 256)
        d_branch = r.d_branch[...].reshape(256, 256)
        hidden = dot(scaled, r.wi[yy], (1, 0)) + r.bias[yy, 0:1, :]
        active, derivative = gelu_parts(hidden)
        active = active.astype(BF16)
        r.branch[...] += dot(active, r.wo[yy], (1, 0))
        r.g_out[dy] = dot(active, d_branch, (0, 0)).astype(BF16)
        d_active = dot(d_branch, r.wo[yy], (1, 1))
        d_hidden = (d_active * derivative).astype(BF16)
        r.g_in[dy] = dot(scaled, d_hidden, (0, 0)).astype(BF16)
        to_core = [
            send(r.g_in.at[dy, :, other_lanes], r.core_in.at[dy], "gc", dy * 2, sibling),
            send(r.g_out.at[dy, other_lanes, :], r.core_out.at[dy], "gc", dy * 2 + 1, sibling),
        ]
        r.d_normed[...] += dot(d_hidden, r.wi[yy], (1, 1))
        return to_core

    def spread(dy, to_core):
        back = (NY - dy) % NY
        to_core[0].wait_recv()
        g_in = r.g_in[dy, :, lanes].astype(F32) + r.core_in[dy].astype(F32)
        r.piece[dy, 0] = g_in[:128].astype(BF16)
        r.piece[dy, 1] = g_in[128:].astype(BF16)
        to_core[1].wait_recv()
        g_out = r.g_out[dy, lanes, :].astype(F32) + r.core_out[dy].astype(F32)
        r.piece[dy, 2] = g_out[:, :128].astype(BF16)
        r.piece[dy, 3] = g_out[:, 128:].astype(BF16)
        for dx in (2, 1, 3, 0):
            if dy or dx:
                index = back * 4 + dx
                send(r.piece.at[dy, (x + dx) % NX], r.piece_in.at[index], "gp", index, plane(back, dx))

    forward_weights(1)
    forward_weights(3)
    pl.semaphore_wait(relay_2, 5)
    first = pair(1)
    second = pair(3)
    spread(1, first)
    spread(3, second)
    forward_weights(2)
    third = pair(2)
    last = pair(0)
    spread(2, third)

    for s in range(SLOTS):
        d_normed = r.d_normed[s * 64:(s + 1) * 64, :] * r.gain[...]
        normed = r.normed[s].reshape(64, 256)
        mean = jnp.mean(d_normed, axis=-1, keepdims=True)
        along = jnp.mean(d_normed * normed, axis=-1, keepdims=True)
        inverse = r.inverse[s].reshape(64, 128)[:, 0:1]
        d_conv = inverse * (d_normed - mean - normed * along)
        r.d_conv[s] = d_conv.astype(BF16).astype(F32).reshape(TH, TW, 256)
    place(r.grid_d, r.d_conv)
    send_edges(r.grid_d, r.edge_d_out, r.edge_d_in, "ed")
    edges = [send(*copy) for copy in edge_copies(r.edge_d_out, r.edge_d_in, "ed")]
    spread(0, last)

    take_edges(r.grid_x, r.edge_x_in)
    for b in range(KS):
        def slot_taps(s, sums):
            sums = list(sums)
            base = r.lats[0, s] * TH
            for i in range(TH + 2 * REACH):
                window = r.grid_x[base + i, LEFT - REACH + b:LEFT - REACH + b + TW, :]
                for a in range(KS):
                    if 0 <= i - a < TH:
                        product = window * r.d_conv[s, i - a]
                        sums[a] += product[:8] + product[8:]
            return tuple(sums)

        sums = lax.fori_loop(
            0, SLOTS, slot_taps, tuple(jnp.zeros((8, 256), F32) for _ in range(KS))
        )
        for a in range(KS):
            line = jnp.sum(sums[a], axis=0, keepdims=True)
            for half in range(2):
                at_row = 2 * (a * KS + b) + half
                owner = at_row // 16
                r.taps[owner % NC, owner // NC, at_row % 16:at_row % 16 + 1, :] = (
                    line[:, half * 128:(half + 1) * 128]
                )
    for at_row in range(2 * KS * KS, 128):
        owner = at_row // 16
        r.taps[owner % NC, owner // NC, at_row % 16:at_row % 16 + 1, :] = jnp.zeros((1, 128), F32)
    k_core = send(r.taps.at[1 - c], r.taps_core, "kc", 0, sibling)
    for s in range(SLOTS):
        r.blocked[s] = (
            (r.cells[s].astype(F32) + r.scale[...] * r.branch[s * 64:(s + 1) * 64, :].reshape(TH, TW, 256))
            * live(s)
        ).astype(BF16)
    give(0, r.blocked, r.blocked_far)
    k_core.wait_recv()
    r.taps_sum[...] = r.taps[c] + r.taps_core[...]
    spot = y * NX + x
    r.taps_plane[spot] = r.taps_sum[y]
    for step in range(1, 16):
        dy, dx = step // 4, step % 4
        send(r.taps_sum.at[(y + dy) % NY], r.taps_plane.at[spot], "kp", step, plane(dy, dx))

    own = r.piece[0, x].astype(F32)
    for step in range(1, 16):
        remote(
            r.piece.at[0, 0], r.piece_in.at[step], "gp", step, plane(step // 4, step % 4)
        ).wait_recv()
        own += r.piece_in[step].astype(F32)
    r.low_out[...] = own.astype(BF16).reshape(NL, 32, 128)
    for dl in (2, 1, 3):
        send(r.low_out.at[(zl + dl) % NL], r.low_in.at[dl], "gl", dl, low(dl))

    for copy in edges:
        copy.wait_recv()
    take_edges(r.grid_d, r.edge_d_in)

    for step in range(1, 16):
        dy, dx = step // 4, step % 4
        origin = (y + NY - dy) % NY * NX + (x + NX - dx) % NX
        remote(r.taps_sum.at[0], r.taps_plane.at[origin], "kp", step, plane(dy, dx)).wait_recv()
    r.taps_low[zl] = jnp.sum(r.taps_plane[...], axis=0)
    for dl in (2, 1, 3):
        send(r.taps_low.at[zl], r.taps_low.at[zl], "kl", dl, low(dl))

    own = r.low_out[zl].astype(F32)
    for dl in range(1, NL):
        remote(r.low_out.at[0], r.low_in.at[dl], "gl", dl, low(dl)).wait_recv()
        own += r.low_in[dl].astype(F32)
    r.high[zh] = own.astype(BF16)
    for dh in (2, 1, 3):
        send(r.high.at[zh], r.high.at[zh], "gh", dh, high(dh))

    for dl in range(1, NL):
        origin = (zl + NL - dl) % NL
        remote(r.taps_low.at[0], r.taps_low.at[origin], "kl", dl, low(dl)).wait_recv()
    r.taps_high[zh] = jnp.sum(r.taps_low[...], axis=0)
    for dh in (2, 1, 3):
        send(r.taps_high.at[zh], r.taps_high.at[zh], "kh", dh, high(dh))

    @pl.loop(0, SLOTS)
    def _(s):
        total = depthwise(r.grid_d, s, True)
        for row in range(TH):
            r.cell_grad[s, row] = (
                (r.cot[s, row].astype(F32) + total[row]) * live(s)
            ).astype(BF16)

    give(1, r.cell_grad, r.cell_grad_far)


    for dh in range(1, NH):
        origin = (zh + NH - dh) % NH
        remote(r.high.at[0], r.high.at[origin], "gh", dh, high(dh)).wait_recv()
    r.full_own[...] = (jnp.sum(r.high[...].astype(F32), axis=0) * factor).astype(BF16)
    for step in range(1, 16):
        dl, dx = step // 4, step % 4
        send(r.full_own, r.full_far.at[x, zl], "gg", step, low(dl, dx))
    give(2, r.full_own, r.full_far.at[x, zl])

    for dh in range(1, NH):
        origin = (zh + NH - dh) % NH
        remote(r.taps_high.at[0], r.taps_high.at[origin], "kh", dh, high(dh)).wait_recv()
    r.taps_own[...] = jnp.sum(r.taps_high[...], axis=0) * factor
    for index in range(1, 8):
        send(r.taps_own, r.taps_full_far.at[m], "km", index, member(index))
    give(3, r.taps_own, r.taps_full_far.at[m])

    for step in range(1, 16):
        dl, dx = step // 4, step % 4
        remote(
            r.full_own,
            r.full_far.at[(x + NX - dx) % NX, (zl + NL - dl) % NL],
            "gg",
            step,
            low(dl, dx),
        ).wait_recv()
    for index in range(1, 8):
        origin = (y + NY - index // NC) % NY * NC + (c + index) % NC
        remote(r.taps_own, r.taps_full_far.at[origin], "km", index, member(index)).wait_recv()
    for copy in sends:
        copy.wait_send()
    for copy in results:
        copy.wait()


def write_kernel(*refs):
    far, out, near = refs[:4], refs[4:9], refs[9:16]
    blocked, cell_grad, full, taps, grad_in, grad_out, kernel_grad = near
    take_sems, give_sems = refs[16:]
    taken = [
        pltpu.make_async_copy(far[index], near[index], take_sems.at[index]) for index in range(4)
    ]
    given = [
        pltpu.make_async_copy(source, out[index], give_sems.at[index])
        for index, source in enumerate((blocked, cell_grad, grad_in, grad_out, kernel_grad))
    ]
    for index in (2, 3, 0, 1):
        taken[index].start()
    taken[2].wait()
    for half in range(2):
        part = slice(half * 128, (half + 1) * 128)
        grad_in[part, :] = full[half].reshape(128, 128).astype(F32)
        grad_out[:, part] = full[2 + half].reshape(128, 128).astype(F32)
    given[2].start()
    given[3].start()
    taken[0].wait()
    given[0].start()
    taken[1].wait()
    given[1].start()
    taken[3].wait()
    for a in range(KS):
        for b in range(KS):
            for half in range(2):
                at_row = 2 * (a * KS + b) + half
                kernel_grad[a, b:b + 1, half * 128:(half + 1) * 128] = (
                    taps[at_row // 16, at_row % 16:at_row % 16 + 1, :]
                )
    given[4].start()
    for copy in given:
        copy.wait()


def on_device(
    cells, cotangent, slot_lats, slot_count, kernel, ln_gain, w_in, b_in, w_out, layer_scale
):
    cell_count = 8 * 256 * TH * TW
    factor = 1.0 / math.sqrt(cell_count)
    vmem = pl.BlockSpec(memory_space=pltpu.VMEM)
    smem = pl.BlockSpec(memory_space=pltpu.SMEM)
    hbm = pl.BlockSpec(memory_space=pltpu.HBM)
    tiles = jax.ShapeDtypeStruct((SLOTS, TH, TW, 256), BF16)
    shapes = (
        tiles,
        tiles,
        jax.ShapeDtypeStruct((256, 128), F32),
        jax.ShapeDtypeStruct((128, 256), F32),
        jax.ShapeDtypeStruct((KS, KS, 256), F32),
    )
    parts = (
        tiles,
        tiles,
        jax.ShapeDtypeStruct((NX, NL, 32, 128), BF16),
        jax.ShapeDtypeStruct((NY * NC, 16, 128), F32),
    )
    results = pl.pallas_call(
        functools.partial(block_kernel, factor),
        out_shape=parts,
        in_specs=[hbm, hbm, smem, smem, hbm, vmem, hbm, vmem, hbm, vmem],
        out_specs=[hbm] * 4,
        scratch_shapes=[pltpu.VMEM(*spec) for spec in VMEM_SCRATCH.values()]
        + [pltpu.SemaphoreType.DMA((n,)) for n in DMA_COUNTS.values() for _ in range(2)]
        + [
            pltpu.SemaphoreType.DMA((len(LOCAL),)),
            pltpu.SemaphoreType.DMA((len(OUTPUTS),)),
            pltpu.SemaphoreType.REGULAR,
            pltpu.SemaphoreType.REGULAR,
        ],
        compiler_params=pltpu.CompilerParams(
            collective_id=0, has_side_effects=True, vmem_limit_bytes=VMEM_BYTES
        ),
        name="block",
    )(
        cells[0],
        cotangent[0],
        slot_lats,
        slot_count,
        kernel,
        ln_gain.reshape(1, 256),
        w_in,
        b_in.reshape(1, 128),
        w_out,
        layer_scale.reshape(1, 256),
    )
    blocked, cell_grad, grad_in, grad_out, kernel_grad = pl.pallas_call(
        write_kernel,
        out_shape=shapes,
        in_specs=[hbm] * 4,
        out_specs=[hbm] * 5,
        scratch_shapes=[pltpu.VMEM(shape.shape, shape.dtype) for shape in parts + shapes[2:]]
        + [pltpu.SemaphoreType.DMA((4,)), pltpu.SemaphoreType.DMA((5,))],
        compiler_params=pltpu.CompilerParams(vmem_limit_bytes=VMEM_BYTES),
        name="write",
    )(*results)
    return blocked[None], cell_grad[None], grad_in, grad_out, kernel_grad


def solution(mesh):
    placed = (
        P("member", "tile", None, None, None),
        P("member", "tile", None, None, None),
        P("tile", None),
        P("tile"),
        P(),
        P(),
        P(None, "member"),
        P("member"),
        P("member", None),
        P(),
    )
    return jax.shard_map(
        on_device,
        mesh=mesh,
        in_specs=placed,
        out_specs=(
            P("member", "tile", None, None, None),
            P("member", "tile", None, None, None),
            P(None, "member"),
            P("member", None),
            P(),
        ),
        check_vma=False,
    )
```
